32 devices in a mesh: dp: 4 (over y, core), ctx: 2 (over x), exp: 4 (over z).
Axes of the slice: x: 2, y: 2, z: 4, core: 2. Of those that a mesh axis runs over, the one named last changes fastest.
Arguments:
- residual: bfloat16 [4, 96, 4096], P('dp', 'ctx', 'exp'), may hold values from -80 to 80
- ssm_input: bfloat16 [4, 96, 4096], P('dp', 'ctx', 'exp'), may hold values from -80 to 80
- ssm_gate: bfloat16 [4, 96, 4096], P('dp', 'ctx', 'exp'), may hold values from -6 to 6
- input_map: bfloat16 [4, 96, 128], P('dp', 'ctx'), may hold values from -2 to 2
- output_map: bfloat16 [4, 96, 128], P('dp', 'ctx'), may hold values from -2 to 2
- step_raw: float32 [4, 96, 64], P('dp', 'ctx', 'exp'), may hold values from -2 to 288
- log_rate: float32 [64], P('exp'), may hold values from -12 to 2
- skip_gain: float32 [64], P('exp'), may hold values from 0.5 to 1.5
- head_gain: float32 [4096], P('exp'), may hold values from 0.1 to 1.9
- moe_gain: float32 [4096], replicated, may hold values from 0.1 to 1.9
- expert_ids: int32 [4, 96, 2], P('dp', 'ctx'), may hold values from 0 to 3, all different within a row; in each aligned block of 12 rows (0 to 11, 12 to 23, ..., all dimensions but the last counted through in order) at most 12 rows name the same one
- gate_weight: float32 [4, 96, 2], P('dp', 'ctx'), may hold values from 0.1 to 1
- expert_up: bfloat16 [4, 4096, 6144], P('exp', None, ('dp', 'ctx')), may hold values from -0.09375 to 0.09375
- expert_down: bfloat16 [4, 6144, 4096], P('exp', ('dp', 'ctx')), may hold values from -0.078125 to 0.078125
Outputs:
- hidden: bfloat16 [4, 96, 4096], P('dp', 'ctx', 'exp')
- moe_out: bfloat16 [4, 96, 4096], P('dp', ('ctx', 'exp'))
The draws below stay inside these ranges and needn't reach their ends.
Inputs may be any that keep to these rules, and one draw needn't show every extreme that they name: `expert_ids`: within each aligned block of 12 positions of one sequence, no expert is named by more than 12 routes; some expert is named by exactly 12 routes in some block; the two routes of a position name different experts.
All inputs are finite; a program needn't handle non-finite values.
Results may differ from the reference program's by a relative error of at most 0.02.
Values may be sent and summed in bfloat16 or wider, within the bound.
No kernel may reach another device: no remote copies, remote signals or barrier semaphores. Data moves between devices by JAX's collectives and lax.ppermute only.
A program may use at most 64 MiB of HBM per device.

```python
import math
import jax
import jax.numpy as jnp
import numpy as np
from jax import lax

HEADS = 64
HEADDIM = 64
STATE = 128
FFD = 768
TOKM = 12
D = 4096
FF = 6144
EXPERTS = 4
BATCH = 4
L_DEV = 48
SEQLEN = 96
CAP = 12
N_DP = 4
N_CTX = 2


def head_rates(key):
    mixed_key = jax.random.fold_in(key, 101)
    order_key, fast_key, slow_key = jax.random.split(mixed_key, 3)
    order = jax.random.permutation(order_key, HEADS)
    quick_channel_count = HEADS // 2
    quick = order < quick_channel_count
    fast_rate = jnp.exp(jax.random.uniform(fast_key, (HEADS,), jnp.float32, math.log(4.0), math.log(6.4))) / L_DEV
    slow_rate = jnp.exp(jax.random.uniform(slow_key, (HEADS,), jnp.float32, math.log(0.2), math.log(0.6))) / SEQLEN
    return (jnp.where(quick, fast_rate, slow_rate), quick)


def spike_mask(key):
    spots = jax.random.randint(jax.random.fold_in(key, 202), (BATCH, 2), 0, SEQLEN)
    positions = jnp.arange(SEQLEN)
    return jnp.any(positions[None, :, None] == spots[:, None, :], axis=2)


def draw_log_rate(key, part):
    rates, quick = head_rates(key)
    return jnp.log(rates)


def draw_step_raw(key, part):
    rates, quick = head_rates(key)
    token_markers = spike_mask(key)
    base_key, stretch_key, strength_key = jax.random.split(jax.random.fold_in(key, 303), 3)
    base = jnp.exp(jax.random.uniform(base_key, (BATCH, SEQLEN, HEADS), jnp.float32, math.log(0.5), 0.0))
    stretch_factor = jnp.exp(jax.random.uniform(stretch_key, (BATCH, SEQLEN // L_DEV, HEADS), jnp.float32, math.log(0.5), math.log(1.5)))
    steps = base * jnp.repeat(stretch_factor, L_DEV, axis=1)
    spike_strength = jnp.exp(jax.random.uniform(strength_key, (BATCH, SEQLEN, HEADS), jnp.float32, math.log(0.22), math.log(0.6)))
    bursting = token_markers[:, :, None] & jnp.logical_not(quick)[None, None, :]
    steps = jnp.where(bursting, spike_strength / rates[None, None, :], steps)
    return steps + jnp.log(-jnp.expm1(-steps))


def draw_ssm_input(key, part):
    rates, quick = head_rates(key)
    token_markers = spike_mask(key)
    noise_key = jax.random.fold_in(jax.random.fold_in(key, 404), 0)
    values = jax.random.normal(noise_key, (BATCH, SEQLEN, D), jnp.float32)
    slow_channel = jnp.repeat(jnp.logical_not(quick), HEADDIM)
    quiet = token_markers[:, :, None] & slow_channel[None, None, :]
    return jnp.where(quiet, 0.04 * values, values).astype(jnp.bfloat16)


def draw_residual(key, part):
    noise_key = jax.random.fold_in(jax.random.fold_in(key, 505), 0)
    values = jax.random.normal(noise_key, (BATCH, SEQLEN, D), jnp.float32)
    return values.astype(jnp.bfloat16)


def levels(rng, shape, shards, least, largest):
    def one(dim, parts):
        draws = jax.random.uniform(jax.random.fold_in(jax.random.fold_in(rng, 6), dim), (parts,), jnp.float32, least / len(shards), largest / len(shards))
        return jnp.repeat(jnp.exp(draws), shape[dim] // parts).reshape((-1,) + (1,) * (len(shape) - dim - 1))

    gain = one(*shards[0])
    for cut in shards[1:]:
        gain = gain * one(*cut)
    return gain


def assign_block(key, own, number, rows, number_of, top, bound, skew):
    order = jax.random.permutation(key, number_of)
    crowded, ordinary = shares(number_of, rows * top, bound, skew, True), shares(number_of, rows * top, bound, skew, False)
    places = jnp.arange(number_of)

    def named(lengths, offset_by):
        used = int((lengths > 0).sum())
        fixed = max(1, used // 4)
        moved = fixed + (places - fixed + offset_by * (used - fixed)) % max(1, number_of - fixed)
        return jnp.zeros((number_of,), jnp.int32).at[order[jnp.where(places < fixed, places, moved)]].set(jnp.asarray(lengths, jnp.int32))

    lengths = jnp.where(number % 4 == 0, named(crowded, number // 4), named(ordinary, number - number // 4 - 1))
    mixed = jax.random.permutation(jax.random.fold_in(own, 3), number_of)
    donor, sink = mixed[0:number_of // 2 * 2:2], mixed[1:number_of // 2 * 2:2]
    room = jnp.minimum(lengths[donor] - 1, bound - lengths[sink]) // 2
    room = jnp.where((donor == order[0]) | (sink == order[0]) | (lengths[sink] == 0), 0, jnp.maximum(room, 0))
    moved = jax.random.randint(jax.random.fold_in(own, 4), (number_of // 2,), 0, 1 << 20) % (room + 1)
    lengths = lengths.at[donor].add(-moved).at[sink].add(moved)
    labels = jnp.searchsorted(jnp.cumsum(lengths), jnp.arange(rows * top), side="right").astype(jnp.int32)
    listing = labels.reshape(top, rows).T
    listing = listing[jax.random.permutation(jax.random.fold_in(own, 1), rows)]
    offset_by = jax.random.randint(jax.random.fold_in(own, 2), (rows, 1), 0, top)
    return jnp.take_along_axis(listing, (jnp.arange(top)[None, :] + offset_by) % top, axis=1)


def shares(number_of, total, bound, skew, full):
    portions = [(1 << 20) // math.isqrt(standing ** skew) + 1 for standing in range(1, number_of + 1)]
    largest = bound if full else min(bound, max(-(-total // number_of), total * portions[0] // sum(portions)))
    least = 1 if total - largest >= number_of - 1 else 0
    given, surplus = [largest] + [least] * (number_of - 1), total - largest - least * (number_of - 1)
    while surplus > 0:
        movable = [i for i in range(1, number_of) if given[i] < largest] or [i for i in range(1, number_of) if given[i] < bound]
        mass, left = sum([portions[i] for i in movable]), surplus
        for i in movable:
            extra = min(bound - given[i], max(1, left * portions[i] // mass), surplus)
            given[i] = given[i] + extra
            surplus = surplus - extra
    return np.array(given)


def gaussian(rng, extent, scale, limit, cuts=(), held_as=jnp.bfloat16):
    array = jax.random.normal(rng, extent, jnp.float32) * scale
    if len(cuts) > 0:
        array = levels(rng, extent, cuts, -0.22, 0.18) * array
    return jnp.clip(array, min=-limit, max=limit).astype(held_as)


def setup_inputs(seed: int = 0) -> dict:
    seeds = jax.random.split(jax.random.key(seed), 15)
    residual = draw_residual(jax.random.fold_in(seeds[14], 71), 0)
    ssm_input = draw_ssm_input(jax.random.fold_in(seeds[14], 71), 0)
    ssm_gate = gaussian(seeds[2], (BATCH, SEQLEN, D), 1.0, 6.0, ((0, 4), (1, 2), (2, 4)))
    input_map = gaussian(seeds[3], (BATCH, SEQLEN, STATE), 0.3, 2.0, ((0, 4), (1, 2)))
    output_map = gaussian(seeds[4], (BATCH, SEQLEN, STATE), 0.3, 2.0, ((0, 4), (1, 2)))
    step_raw = draw_step_raw(jax.random.fold_in(seeds[14], 71), 0)
    log_rate = draw_log_rate(jax.random.fold_in(seeds[14], 71), 0)
    skip_gain = jnp.clip(0.5 + 1.0 * jax.random.uniform(seeds[7], (HEADS,), jnp.float32) ** levels(seeds[7], (HEADS,), ((0, 4),), -0.2, 0.2), 0.5, 1.5)
    head_gain = jnp.clip(1.0 + 0.18 * jax.random.normal(seeds[8], (D,), jnp.float32), 0.1, 1.9)
    moe_gain = jnp.clip(1.0 + 0.18 * jax.random.normal(seeds[9], (D,), jnp.float32), 0.1, 1.9)
    expert_ids_keys = jax.random.split(jax.random.fold_in(seeds[10], 1), BATCH * SEQLEN // TOKM)
    expert_ids_turns = jax.random.permutation(jax.random.fold_in(seeds[10], 3), BATCH * SEQLEN // TOKM)
    expert_ids = jax.vmap(lambda own, number: assign_block(jax.random.fold_in(seeds[10], 2), own, number, TOKM, EXPERTS, 2, CAP, 3))(expert_ids_keys, expert_ids_turns).reshape((BATCH, SEQLEN, 2))
    gate_weight = jnp.clip(0.1 + 0.9 * jax.random.uniform(seeds[11], (BATCH, SEQLEN, 2), jnp.float32) ** levels(seeds[11], (BATCH, SEQLEN, 2), ((0, 4), (1, 2)), -0.2, 0.2), 0.1, 1.0)
    expert_up = gaussian(seeds[12], (EXPERTS, D, FF), D ** -0.5, 0.09375, ((0, 4), (2, 8)))
    expert_down = gaussian(seeds[13], (EXPERTS, FF, D), FF ** -0.5, 0.078125, ((0, 4), (1, 8)))
    return dict(residual=residual, ssm_input=ssm_input, ssm_gate=ssm_gate, input_map=input_map, output_map=output_map, step_raw=step_raw, log_rate=log_rate, skip_gain=skip_gain, head_gain=head_gain, moe_gain=moe_gain, expert_ids=expert_ids, gate_weight=gate_weight, expert_up=expert_up, expert_down=expert_down)


EPSILON = 1e-05

def route_slots(routes, experts):
    blocks = routes.shape[0]
    ordered = routes.reshape(blocks, -1)
    matches = (ordered[:, :, None] == jnp.arange(experts, dtype=jnp.int32)[None, None, :]).astype(jnp.int32)
    earlier = jnp.cumsum(matches, axis=1) - matches
    return lax.optimization_barrier(jnp.sum(earlier * matches, axis=2)).reshape(routes.shape).astype(jnp.int32)

def reference(residual, ssm_input, ssm_gate, input_map, output_map, step_raw, log_rate, skip_gain, head_gain, moe_gain, expert_ids, gate_weight, expert_up, expert_down):
    step_size = jax.nn.softplus(step_raw)
    cumulative = jnp.cumsum(step_size * (-jnp.exp(log_rate))[None, None, :], axis=1)
    values = ssm_input.astype(jnp.float32).reshape(BATCH, SEQLEN, HEADS, HEADDIM)
    positions = jnp.arange(SEQLEN)
    causal = positions[:, None] >= positions[None, :]

    def one_sequence(operands):
        cum_seq, in_map, out_map, steps_seq, values_seq = operands
        scores = jnp.dot(out_map, in_map.T, preferred_element_type=jnp.float32)

        def one_head(head_ops):
            cum_head, step_head, values_head = head_ops
            spread = cum_head[:, None] - cum_head[None, :]
            kernel = jnp.where(causal, jnp.exp(jnp.minimum(spread, 0.0)), 0.0) * scores * step_head[None, :]
            return jnp.dot(kernel, values_head, precision=lax.Precision.HIGHEST)
        return lax.map(one_head, (cum_seq.T, steps_seq.T, jnp.transpose(values_seq, (1, 0, 2))))
    per_head = lax.map(one_sequence, (cumulative, input_map, output_map, step_size, values))
    mixed_y = jnp.transpose(per_head, (0, 2, 1, 3)) + skip_gain[None, None, :, None] * values
    gates = jax.nn.silu(ssm_gate.astype(jnp.float32).reshape(BATCH, SEQLEN, HEADS, HEADDIM))
    gated = mixed_y * gates
    normed = gated * lax.rsqrt(lax.optimization_barrier(jnp.mean(gated * gated, axis=3, keepdims=True)) + EPSILON) * head_gain.reshape(HEADS, HEADDIM)
    hidden = (residual.astype(jnp.float32) + normed.reshape(BATCH, SEQLEN, D)).astype(jnp.bfloat16)
    hidden_wide = hidden.astype(jnp.float32)
    normal_rows = (hidden_wide * lax.rsqrt(lax.optimization_barrier(jnp.mean(hidden_wide * hidden_wide, axis=2, keepdims=True)) + EPSILON) * moe_gain[None, None, :]).astype(jnp.bfloat16)
    blocks = BATCH * SEQLEN // TOKM
    routes = expert_ids.reshape(blocks, TOKM, 2)
    slots = route_slots(routes, EXPERTS)
    block_ids = jnp.broadcast_to(jnp.arange(blocks, dtype=jnp.int32)[:, None, None], routes.shape)
    rows_in = jnp.broadcast_to(normal_rows.reshape(blocks, TOKM, 1, D), (blocks, TOKM, 2, D))
    buffer = jnp.zeros((EXPERTS, blocks, CAP, D), jnp.bfloat16).at[routes, block_ids, slots].set(rows_in)
    groups = N_DP * N_CTX

    def one_expert(operands):
        rows_expert, up_expert, down_expert = operands
        activated = jax.nn.silu(jnp.dot(rows_expert, up_expert, preferred_element_type=jnp.float32)).astype(jnp.bfloat16)
        row_count = activated.shape[0]
        act_groups = jnp.transpose(activated.reshape(row_count, groups, FFD), (1, 0, 2))
        down_groups = down_expert.reshape(groups, FFD, D)

        def add_group(total, group_operations):
            act_part, down_part = group_operations
            partial_sum = jnp.dot(act_part, down_part, preferred_element_type=jnp.float32).astype(jnp.bfloat16)
            partial_sum = lax.optimization_barrier(partial_sum)
            return (total + partial_sum.astype(jnp.float32), None)
        total, unused = lax.scan(add_group, jnp.zeros((row_count, D), jnp.float32), (act_groups, down_groups))
        return total.astype(jnp.bfloat16)
    outputs = lax.map(one_expert, (buffer.reshape(EXPERTS, blocks * CAP, D), expert_up, expert_down))
    outputs = outputs.reshape(EXPERTS, blocks, CAP, D)
    picked = outputs[routes, block_ids, slots].astype(jnp.float32)
    combined = lax.optimization_barrier(jnp.sum(gate_weight.reshape(blocks, TOKM, 2)[:, :, :, None] * picked, axis=2))
    moe_out = combined.astype(jnp.bfloat16).reshape(BATCH, SEQLEN, D)
    return (hidden, moe_out)
```

```python
import functools

import jax
import jax.numpy as jnp
from jax import lax
from jax.experimental import pallas as pl
from jax.experimental.pallas import tpu as pltpu
from jax.sharding import PartitionSpec as P

EPSILON = 1e-05
BF16 = jnp.bfloat16
F32 = jnp.float32
MIB = 1 << 20


def shifted(block, axis, distance):
    devices = range(lax.axis_size(axis))
    route = [(i - distance, i) for i in devices if i - distance in devices]
    return lax.ppermute(block, axis, route)


def route_slots(routes, experts):
    blocks = routes.shape[0]
    ordered = routes.reshape(blocks, -1)
    matches = (ordered[:, :, None] == jnp.arange(experts, dtype=jnp.int32)[None, None, :]).astype(
        jnp.int32
    )
    earlier = jnp.cumsum(matches, axis=1) - matches
    return jnp.sum(earlier * matches, axis=2).reshape(routes.shape)


def body(
    residual,
    ssm_input,
    ssm_gate,
    input_map,
    output_map,
    step_raw,
    log_rate,
    skip_gain,
    head_gain,
    moe_gain,
    expert_ids,
    gate_weight,
    expert_up,
    expert_down,
):
    heads_loc = log_rate.shape[0]
    local_rows = residual.shape[1]
    width_loc = residual.shape[2]
    head_size = width_loc // heads_loc
    values = ssm_input[0].astype(jnp.float32).reshape(local_rows, heads_loc, head_size)
    step_size = jax.nn.softplus(step_raw[0])
    cumulative = jnp.cumsum(step_size * (-jnp.exp(log_rate))[None, :], axis=0)
    scores = jnp.einsum(
        "tn,sn->ts", output_map[0], input_map[0], preferred_element_type=jnp.float32
    )
    positions = jnp.arange(local_rows)
    causal = positions[:, None] >= positions[None, :]
    spread = cumulative[:, None, :] - cumulative[None, :, :]
    kernel = (
        jnp.where(causal[:, :, None], jnp.exp(jnp.minimum(spread, 0.0)), 0.0)
        * scores[:, :, None]
        * step_size[None, :, :]
    )
    within = jnp.einsum("tsh,shp->thp", kernel, values, precision=lax.Precision.HIGHEST)
    ending = cumulative[-1]
    carried = jnp.exp(ending[None, :] - cumulative) * step_size
    in_map_wide = input_map[0].astype(jnp.float32)
    out_map_wide = output_map[0].astype(jnp.float32)
    local_state = jnp.einsum(
        "sh,shp,sn->hpn", carried, values, in_map_wide, precision=lax.Precision.HIGHEST
    )
    total_decay = jnp.exp(ending)
    incoming = jnp.zeros_like(local_state)
    for repeat in range(lax.axis_size("ctx") - 1):
        outgoing = total_decay[:, None, None] * incoming + local_state
        incoming = shifted(outgoing.astype(jnp.bfloat16), "ctx", 1).astype(outgoing.dtype)
    across_heads = (
        jnp.einsum("tn,hpn->thp", out_map_wide, incoming, precision=lax.Precision.HIGHEST)
        * jnp.exp(cumulative)[:, :, None]
    )
    mixed_y = within + across_heads + skip_gain[None, :, None] * values
    gated = mixed_y * jax.nn.silu(
        ssm_gate[0].astype(jnp.float32).reshape(local_rows, heads_loc, head_size)
    )
    normed = (
        gated
        * lax.rsqrt(jnp.mean(gated * gated, axis=2, keepdims=True) + EPSILON)
        * head_gain.reshape(heads_loc, head_size)
    )
    hidden = (residual[0].astype(jnp.float32) + normed.reshape(local_rows, width_loc)).astype(
        jnp.bfloat16
    )
    exp_count = lax.axis_size("exp")
    my_expert = lax.axis_index("exp")
    tok_rows = local_rows // exp_count
    capacity = min(tok_rows, max(4, 4 * tok_rows // exp_count))
    model_width = width_loc * exp_count
    routes_all = expert_ids[0].reshape(exp_count, tok_rows, 2)
    slots_all = route_slots(routes_all, exp_count)
    targets_all = routes_all * capacity + slots_all
    slot_ids = jnp.arange(exp_count * capacity, dtype=jnp.int32)
    own_targets = lax.dynamic_slice_in_dim(targets_all, my_expert, 1, 0)[0]
    own_weights = lax.dynamic_slice_in_dim(
        gate_weight[0].reshape(exp_count, tok_rows, 2), my_expert, 1, 0
    )[0]
    hidden_wide = hidden.astype(jnp.float32)
    squared_values = lax.psum(jnp.sum(hidden_wide * hidden_wide, axis=1), "exp")
    gain_part = lax.dynamic_slice_in_dim(moe_gain, my_expert * width_loc, width_loc, 0)
    normal_part = (
        hidden_wide
        * lax.rsqrt(squared_values[:, None] / model_width + EPSILON)
        * gain_part[None, :]
    ).astype(jnp.bfloat16)
    placing_all = jnp.any(
        slot_ids[None, :, None, None] == targets_all[:, None, :, :], axis=3
    ).astype(jnp.bfloat16)
    outbound = jnp.einsum(
        "bqt,btc->bqc",
        placing_all,
        normal_part.reshape(exp_count, tok_rows, width_loc),
        preferred_element_type=jnp.float32,
    )
    outbound = outbound.astype(jnp.bfloat16).reshape(exp_count, exp_count, capacity, width_loc)
    arrived = lax.all_to_all(outbound, "exp", split_axis=1, concat_axis=3, tiled=True).reshape(
        exp_count * capacity, model_width
    )
    up_local = expert_up[0]
    down_local = expert_down[0]
    activated = jax.nn.silu(
        jnp.dot(
            lax.all_gather(arrived, ("dp", "ctx"), axis=0, tiled=True),
            up_local,
            preferred_element_type=jnp.float32,
        )
    ).astype(jnp.bfloat16)
    summed = lax.psum_scatter(
        jnp.dot(activated, down_local, preferred_element_type=jnp.float32).astype(jnp.bfloat16),
        ("dp", "ctx"),
        scatter_dimension=0,
        tiled=True,
    )
    sent_back = summed.reshape(exp_count, capacity, model_width)
    returned = lax.all_to_all(sent_back, "exp", split_axis=0, concat_axis=0, tiled=True).reshape(
        exp_count * capacity, model_width
    )
    picking = (own_targets.reshape(-1)[:, None] == slot_ids[None, :]).astype(jnp.bfloat16)
    chosen = jnp.dot(picking, returned, preferred_element_type=jnp.float32).reshape(
        tok_rows, 2, model_width
    )
    combined = jnp.sum(own_weights[:, :, None] * chosen, axis=1).astype(jnp.bfloat16)
    return (hidden[None], combined[None])


def mixer_kernel(
    x_ref, xp_ref, small_ref, gate_ref, res_ref, b_ref, c_ref, step_ref, rate_ref, gain_ref, skip_ref, out_ref
):
    rows, width = x_ref.shape
    heads = step_ref.shape[1]
    size = width // heads
    pad = 64 - rows
    state = b_ref.shape[1]
    zeros = jnp.zeros((pad, heads), F32)
    steps = jnp.concatenate([small_ref[:, state:], zeros, step_ref[...], zeros], axis=0)
    steps = jnp.maximum(steps, 0.0) + jnp.log1p(jnp.exp(-jnp.abs(steps)))
    where_row = lax.broadcasted_iota(jnp.int32, (128, heads), 0)
    steps = jnp.where((where_row & 63) < rows, steps, 0.0)
    decay = steps * (-jnp.exp(rate_ref[...]))
    wide = jnp.concatenate([decay, steps, jnp.zeros((128, 128 - 2 * heads), F32)], axis=1)
    flipped = wide.T
    decay_t, steps_t = flipped[:heads], flipped[heads : 2 * heads]
    u_row = lax.broadcasted_iota(jnp.int32, (128, 128), 0)
    s_col = lax.broadcasted_iota(jnp.int32, (128, 128), 1)
    before = (u_row < 64) & (s_col < 64) & (u_row > s_col)
    inside = (u_row >= 64) & (s_col >= 64) & (u_row <= s_col)
    to_row = jnp.where(before, 1.0, 0.0) - jnp.where(inside, 1.0, 0.0)
    row_part = jnp.dot(decay_t, to_row, precision=lax.Precision.HIGHEST, preferred_element_type=F32)
    t_row = lax.broadcasted_iota(jnp.int32, (rows, 128), 0) + 64
    u_col = lax.broadcasted_iota(jnp.int32, (rows, 128), 1)
    to_col = jnp.where((u_col >= 64) & (u_col <= t_row), 1.0, 0.0)
    col_part = jnp.dot(to_col, decay, precision=lax.Precision.HIGHEST, preferred_element_type=F32)
    zeros_b = jnp.zeros((pad, state), BF16)
    maps = jnp.concatenate([small_ref[:, :state].astype(BF16), zeros_b, b_ref[...], zeros_b], axis=0)
    scores = lax.dot_general(c_ref[...], maps, (((1,), (1,)), ((), ())), preferred_element_type=F32)
    scores = jnp.where(u_col <= t_row, scores, 0.0)
    lane = lax.broadcasted_iota(jnp.int32, (1, 128), 1)
    low = lane < size
    zeros_x = jnp.zeros((pad, 128), BF16)
    for pair in range(width // 128):
        cut = slice(pair * 128, (pair + 1) * 128)
        x_own = x_ref[:, cut]
        x_all = jnp.concatenate([xp_ref[:, cut], zeros_x, x_own, zeros_x], axis=0)
        left, right = [], []
        for h in (2 * pair, 2 * pair + 1):
            spread = jnp.minimum(col_part[:, h : h + 1] + row_part[h : h + 1], 0.0)
            kernel = jnp.exp(spread) * scores * steps_t[h : h + 1]
            high = kernel.astype(BF16)
            rest = (kernel - high.astype(F32)).astype(BF16)
            left.append(jnp.concatenate([high, rest], axis=0))
            mine = low if h % 2 == 0 else jnp.logical_not(low)
            right.append(jnp.where(mine, x_all, jnp.zeros_like(x_all)))
        mixed = jnp.dot(
            jnp.concatenate(left, axis=1), jnp.concatenate(right, axis=0), preferred_element_type=F32
        )
        skip = jnp.where(low, skip_ref[2 * pair], skip_ref[2 * pair + 1])
        mixed = mixed[:rows] + mixed[rows:] + skip * x_own.astype(F32)
        gate = gate_ref[:, cut].astype(F32)
        gated = mixed * (gate / (1.0 + jnp.exp(-gate)))
        square = gated * gated
        mean_low = jnp.sum(jnp.where(low, square, 0.0), axis=1, keepdims=True) / size
        mean_high = jnp.sum(jnp.where(low, 0.0, square), axis=1, keepdims=True) / size
        scale = lax.rsqrt(jnp.where(low, mean_low, mean_high) + EPSILON)
        normed = gated * scale * gain_ref[:, cut]
        out_ref[:, cut] = (res_ref[:, cut].astype(F32) + normed).astype(BF16)


def norm_kernel(expert, parts, *refs):
    pieces, gain_ref, out_ref = refs[:parts], refs[parts], refs[parts + 1]
    me = lax.axis_index(expert)
    width = pieces[0].shape[1]
    wide = [piece[...].astype(F32) for piece in pieces]
    total = sum(jnp.sum(w * w, axis=1, keepdims=True) for w in wide)
    scale = lax.rsqrt(total / (parts * width) + EPSILON)
    for k in range(parts):
        gain = gain_ref[pl.ds(me ^ k, 1), :]
        out_ref[:, k * width : (k + 1) * width] = (wide[k] * scale * gain).astype(BF16)


def up_kernel(blocks, *refs):
    rows, up_ref, out_ref, total = refs[:blocks], refs[blocks], refs[blocks + 1], refs[blocks + 2]
    step = pl.program_id(0)
    wide = jnp.concatenate([r[...] for r in rows], axis=0)
    part = jnp.dot(wide, up_ref[...], preferred_element_type=F32)

    @pl.when(step == 0)
    def _():
        total[...] = part

    @pl.when(step > 0)
    def _():
        total[...] += part

    @pl.when(step == pl.num_programs(0) - 1)
    def _():
        value = total[...]
        out_ref[...] = (value / (1.0 + jnp.exp(-value))).astype(BF16)


def down_kernel(act_ref, down_ref, out_ref):
    out_ref[...] = jnp.dot(act_ref[...], down_ref[...], preferred_element_type=F32).astype(BF16)


def weigh_kernel(expert, own_ref, *refs):
    others, ids_ref, weight_ref, outs = refs[:3], refs[3], refs[4], refs[5:]
    me = lax.axis_index(expert)
    rows = own_ref.shape[0]
    keep = outs[0].shape[0]
    total = own_ref[...].astype(F32)
    for other in others:
        total += other[...].astype(F32)
    weight = jnp.sum(jnp.where(ids_ref[...] == me, weight_ref[...], 0.0), axis=1, keepdims=True)
    total = (total * weight).astype(BF16)
    place = lax.broadcasted_iota(jnp.int32, (16 * len(outs), rows), 0)
    source = lax.broadcasted_iota(jnp.int32, (16 * len(outs), rows), 1)
    wanted = ((place // 16) ^ me) * keep + place % 16
    pick = jnp.where((place % 16 < keep) & (source == wanted), 1.0, 0.0).astype(BF16)
    picked = jnp.dot(pick, total, preferred_element_type=F32)
    for k, out in enumerate(outs):
        out[...] = picked[16 * k : 16 * k + keep].astype(BF16)


def plane_body(
    residual, ssm_input, ssm_gate, input_map, output_map, step_raw, log_rate, skip_gain, head_gain,
    moe_gain, expert_ids, gate_weight, expert_up, expert_down,
):
    rows, width = residual.shape[1:]
    state = input_map.shape[2]
    experts = lax.axis_size("exp")
    model = experts * width
    hidden_units = expert_up.shape[2]
    me = lax.axis_index("exp")
    plane = ("dp", "ctx")
    small = jnp.concatenate([input_map[0].astype(F32), step_raw[0]], axis=1)
    x_before = lax.ppermute(ssm_input[0], "ctx", [(0, 1)])
    small_before = lax.ppermute(small, "ctx", [(0, 1)])
    vmem = pl.BlockSpec(memory_space=pltpu.VMEM)
    hidden = pl.pallas_call(
        mixer_kernel,
        out_shape=jax.ShapeDtypeStruct((rows, width), BF16),
        in_specs=[vmem] * 10 + [pl.BlockSpec(memory_space=pltpu.SMEM)],
        out_specs=vmem,
        compiler_params=pltpu.CompilerParams(vmem_limit_bytes=16 * MIB),
        name="mixer",
    )(
        ssm_input[0], x_before, small_before, ssm_gate[0], residual[0], input_map[0], output_map[0],
        step_raw[0], log_rate[None], head_gain[None], skip_gain,
    )

    def along_z(block, k):
        return lax.ppermute(block, "exp", [(i, i ^ k) for i in range(experts)])

    def in_plane(block, x, y, core):
        route = [
            (d * 2 + c, (d ^ (y * 2) ^ core) * 2 + (c ^ x)) for d in range(4) for c in range(2)
        ]
        return lax.ppermute(block, plane, route)

    pieces = [hidden] + [along_z(hidden, k) for k in range(1, experts)]
    normal = pl.pallas_call(
        functools.partial(norm_kernel, "exp", experts),
        out_shape=jax.ShapeDtypeStruct((rows, model), BF16),
        in_specs=[vmem] * (experts + 1),
        out_specs=vmem,
        compiler_params=pltpu.CompilerParams(vmem_limit_bytes=16 * MIB),
        name="norm",
    )(*pieces, moe_gain.reshape(experts, width))
    chips = ((0, 0), (1, 0), (0, 1), (1, 1))
    mine = [normal] + [in_plane(normal, x, y, 0) for x, y in chips[1:]]
    sibling = [in_plane(block, 0, 0, 1) for block in mine]
    blocks = mine + sibling
    count = len(blocks) * rows
    activated = pl.pallas_call(
        functools.partial(up_kernel, len(blocks)),
        out_shape=jax.ShapeDtypeStruct((count, hidden_units), BF16),
        grid=(experts,),
        in_specs=[pl.BlockSpec((rows, width), lambda k: (0, k))] * len(blocks)
        + [pl.BlockSpec((width, hidden_units), lambda k: (lax.axis_index("exp") ^ k, 0))],
        out_specs=pl.BlockSpec((count, hidden_units), lambda k: (0, 0)),
        scratch_shapes=[pltpu.VMEM((count, hidden_units), F32)],
        compiler_params=pltpu.CompilerParams(vmem_limit_bytes=32 * MIB),
        name="up",
    )(*blocks, expert_up[0])
    cut = 1024
    partial = pl.pallas_call(
        down_kernel,
        out_shape=jax.ShapeDtypeStruct((count, model), BF16),
        grid=(model // cut,),
        in_specs=[
            pl.BlockSpec((count, hidden_units), lambda n: (0, 0)),
            pl.BlockSpec((hidden_units, cut), lambda n: (0, n)),
        ],
        out_specs=pl.BlockSpec((count, cut), lambda n: (0, n)),
        compiler_params=pltpu.CompilerParams(vmem_limit_bytes=32 * MIB),
        name="down",
    )(activated, expert_down[0])
    half = count // 2
    arrived = in_plane(partial[half:], 0, 0, 1)
    summed = (partial[:half].astype(F32) + arrived.astype(F32)).astype(BF16)
    summed = summed.reshape(4, rows, model)
    returned = [in_plane(summed[i + 1], x, y, 0) for i, (x, y) in enumerate(chips[1:])]
    keep = rows // experts
    slices = pl.pallas_call(
        functools.partial(weigh_kernel, "exp"),
        out_shape=[jax.ShapeDtypeStruct((keep, model), BF16)] * experts,
        in_specs=[vmem] * 6,
        out_specs=[vmem] * experts,
        compiler_params=pltpu.CompilerParams(vmem_limit_bytes=16 * MIB),
        name="weigh",
    )(summed[0], *returned, expert_ids[0], gate_weight[0])
    final = slices[0].astype(F32)
    for k in range(1, experts):
        final += along_z(slices[k], k).astype(F32)
    return (hidden[None], final.astype(BF16)[None])


def solution(mesh):
    placed = (
        P("dp", "ctx", "exp"),
        P("dp", "ctx", "exp"),
        P("dp", "ctx", "exp"),
        P("dp", "ctx", None),
        P("dp", "ctx", None),
        P("dp", "ctx", "exp"),
        P("exp"),
        P("exp"),
        P("exp"),
        P(),
        P("dp", "ctx", None),
        P("dp", "ctx", None),
        P("exp", None, ("dp", "ctx")),
        P("exp", ("dp", "ctx"), None),
    )
    sizes = tuple(mesh.shape[axis] for axis in ("dp", "ctx", "exp"))
    return jax.shard_map(
        plane_body if sizes == (4, 2, 4) else body,
        mesh=mesh,
        in_specs=placed,
        out_specs=(P("dp", "ctx", "exp"), P("dp", ("ctx", "exp"), None)),
        check_vma=False,
    )
```

```python
import functools

import jax
import jax.numpy as jnp
from jax import lax
from jax.experimental import pallas as pl
from jax.experimental.pallas import tpu as pltpu
from jax.sharding import PartitionSpec as P

EPSILON = 1e-05
BF16 = jnp.bfloat16
F32 = jnp.float32
MIB = 1 << 20
EXACT = lax.Precision.HIGHEST
LAST = (((1,), (1,)), ((), ()))


def shifted(block, axis, distance):
    devices = range(lax.axis_size(axis))
    route = [(i - distance, i) for i in devices if i - distance in devices]
    return lax.ppermute(block, axis, route)


def route_slots(routes, experts):
    blocks = routes.shape[0]
    ordered = routes.reshape(blocks, -1)
    matches = (ordered[:, :, None] == jnp.arange(experts, dtype=jnp.int32)[None, None, :]).astype(
        jnp.int32
    )
    earlier = jnp.cumsum(matches, axis=1) - matches
    return jnp.sum(earlier * matches, axis=2).reshape(routes.shape)


def body(
    residual,
    ssm_input,
    ssm_gate,
    input_map,
    output_map,
    step_raw,
    log_rate,
    skip_gain,
    head_gain,
    moe_gain,
    expert_ids,
    gate_weight,
    expert_up,
    expert_down,
):
    heads_loc = log_rate.shape[0]
    local_rows = residual.shape[1]
    width_loc = residual.shape[2]
    head_size = width_loc // heads_loc
    values = ssm_input[0].astype(jnp.float32).reshape(local_rows, heads_loc, head_size)
    step_size = jax.nn.softplus(step_raw[0])
    cumulative = jnp.cumsum(step_size * (-jnp.exp(log_rate))[None, :], axis=0)
    scores = jnp.einsum(
        "tn,sn->ts", output_map[0], input_map[0], preferred_element_type=jnp.float32
    )
    positions = jnp.arange(local_rows)
    causal = positions[:, None] >= positions[None, :]
    spread = cumulative[:, None, :] - cumulative[None, :, :]
    kernel = (
        jnp.where(causal[:, :, None], jnp.exp(jnp.minimum(spread, 0.0)), 0.0)
        * scores[:, :, None]
        * step_size[None, :, :]
    )
    within = jnp.einsum("tsh,shp->thp", kernel, values, precision=lax.Precision.HIGHEST)
    ending = cumulative[-1]
    carried = jnp.exp(ending[None, :] - cumulative) * step_size
    in_map_wide = input_map[0].astype(jnp.float32)
    out_map_wide = output_map[0].astype(jnp.float32)
    local_state = jnp.einsum(
        "sh,shp,sn->hpn", carried, values, in_map_wide, precision=lax.Precision.HIGHEST
    )
    total_decay = jnp.exp(ending)
    incoming = jnp.zeros_like(local_state)
    for repeat in range(lax.axis_size("ctx") - 1):
        outgoing = total_decay[:, None, None] * incoming + local_state
        incoming = shifted(outgoing.astype(jnp.bfloat16), "ctx", 1).astype(outgoing.dtype)
    across_heads = (
        jnp.einsum("tn,hpn->thp", out_map_wide, incoming, precision=lax.Precision.HIGHEST)
        * jnp.exp(cumulative)[:, :, None]
    )
    mixed_y = within + across_heads + skip_gain[None, :, None] * values
    gated = mixed_y * jax.nn.silu(
        ssm_gate[0].astype(jnp.float32).reshape(local_rows, heads_loc, head_size)
    )
    normed = (
        gated
        * lax.rsqrt(jnp.mean(gated * gated, axis=2, keepdims=True) + EPSILON)
        * head_gain.reshape(heads_loc, head_size)
    )
    hidden = (residual[0].astype(jnp.float32) + normed.reshape(local_rows, width_loc)).astype(
        jnp.bfloat16
    )
    exp_count = lax.axis_size("exp")
    my_expert = lax.axis_index("exp")
    tok_rows = local_rows // exp_count
    capacity = min(tok_rows, max(4, 4 * tok_rows // exp_count))
    model_width = width_loc * exp_count
    routes_all = expert_ids[0].reshape(exp_count, tok_rows, 2)
    slots_all = route_slots(routes_all, exp_count)
    targets_all = routes_all * capacity + slots_all
    slot_ids = jnp.arange(exp_count * capacity, dtype=jnp.int32)
    own_targets = lax.dynamic_slice_in_dim(targets_all, my_expert, 1, 0)[0]
    own_weights = lax.dynamic_slice_in_dim(
        gate_weight[0].reshape(exp_count, tok_rows, 2), my_expert, 1, 0
    )[0]
    hidden_wide = hidden.astype(jnp.float32)
    squared_values = lax.psum(jnp.sum(hidden_wide * hidden_wide, axis=1), "exp")
    gain_part = lax.dynamic_slice_in_dim(moe_gain, my_expert * width_loc, width_loc, 0)
    normal_part = (
        hidden_wide
        * lax.rsqrt(squared_values[:, None] / model_width + EPSILON)
        * gain_part[None, :]
    ).astype(jnp.bfloat16)
    placing_all = jnp.any(
        slot_ids[None, :, None, None] == targets_all[:, None, :, :], axis=3
    ).astype(jnp.bfloat16)
    outbound = jnp.einsum(
        "bqt,btc->bqc",
        placing_all,
        normal_part.reshape(exp_count, tok_rows, width_loc),
        preferred_element_type=jnp.float32,
    )
    outbound = outbound.astype(jnp.bfloat16).reshape(exp_count, exp_count, capacity, width_loc)
    arrived = lax.all_to_all(outbound, "exp", split_axis=1, concat_axis=3, tiled=True).reshape(
        exp_count * capacity, model_width
    )
    up_local = expert_up[0]
    down_local = expert_down[0]
    activated = jax.nn.silu(
        jnp.dot(
            lax.all_gather(arrived, ("dp", "ctx"), axis=0, tiled=True),
            up_local,
            preferred_element_type=jnp.float32,
        )
    ).astype(jnp.bfloat16)
    summed = lax.psum_scatter(
        jnp.dot(activated, down_local, preferred_element_type=jnp.float32).astype(jnp.bfloat16),
        ("dp", "ctx"),
        scatter_dimension=0,
        tiled=True,
    )
    sent_back = summed.reshape(exp_count, capacity, model_width)
    returned = lax.all_to_all(sent_back, "exp", split_axis=0, concat_axis=0, tiled=True).reshape(
        exp_count * capacity, model_width
    )
    picking = (own_targets.reshape(-1)[:, None] == slot_ids[None, :]).astype(jnp.bfloat16)
    chosen = jnp.dot(picking, returned, preferred_element_type=jnp.float32).reshape(
        tok_rows, 2, model_width
    )
    combined = jnp.sum(own_weights[:, :, None] * chosen, axis=1).astype(jnp.bfloat16)
    return (hidden[None], combined[None])


def softplus(raw):
    return jnp.maximum(raw, 0.0) + jnp.log1p(jnp.exp(-jnp.abs(raw)))


def iotas(rows, columns):
    shape = (rows, columns)
    return lax.broadcasted_iota(jnp.int32, shape, 0), lax.broadcasted_iota(jnp.int32, shape, 1)


def as_column(row):
    size = row.shape[1]
    down, across = iotas(size, size)
    return jnp.sum(jnp.where(down == across, row, 0.0), axis=1, keepdims=True)


def fetch(pairs, sems):
    copies = [pltpu.make_async_copy(a, b, sems.at[i]) for i, (a, b) in enumerate(pairs)]
    for copy in copies:
        copy.start()
    return copies


def own_kernel(
    x_hbm, gate_hbm, res_hbm, b_hbm, c_hbm, step_hbm, rate_hbm, gain_hbm, skip_hbm,
    mixed_ref, gate_ref, decay_ref, res_ref, c_ref, rate_ref, gain_ref,
    x_ref, raw_gate_ref, b_ref, step_ref, skip_ref, sems,
):
    copies = fetch(
        [
            (step_hbm, step_ref), (rate_hbm, rate_ref), (b_hbm, b_ref), (c_hbm, c_ref), (x_hbm, x_ref),
            (skip_hbm, skip_ref), (gate_hbm, raw_gate_ref), (res_hbm, res_ref), (gain_hbm, gain_ref),
        ],
        sems,
    )
    rows, width = x_ref.shape
    heads = step_ref.shape[0]
    size = width // heads
    pad = 64 - rows
    copies[0].wait()
    copies[1].wait()
    steps = softplus(step_ref[...])
    decay = steps * -jnp.exp(as_column(rate_ref[...]))
    down, across = iotas(rows, 128)
    place = across & 63
    to_row = jnp.where((down <= place) & (place < rows), -1.0, 0.0)
    to_step = jnp.where(down == place, 1.0, 0.0)
    row_part = jnp.dot(decay, to_row, precision=EXACT, preferred_element_type=F32)
    steps_twice = jnp.dot(steps, to_step, precision=EXACT, preferred_element_type=F32)
    t_row, u_col = iotas(rows, rows)
    to_col = jnp.where(u_col <= t_row, 1.0, 0.0)
    col_part = lax.dot_general(to_col, decay, LAST, precision=EXACT, preferred_element_type=F32)
    copies[2].wait()
    copies[3].wait()
    zeros = jnp.zeros((pad, b_ref.shape[1]), BF16)
    maps = jnp.concatenate([b_ref[...], zeros, b_ref[...], zeros], axis=0)
    scores = lax.dot_general(c_ref[...], maps, LAST, preferred_element_type=F32)
    scores = jnp.where(place <= down, scores, 0.0)
    lane = lax.broadcasted_iota(jnp.int32, (1, 128), 1)
    low = lane < size
    zeros = jnp.zeros((pad, 128), BF16)
    for copy in copies[4:]:
        copy.wait()
    skips = as_column(skip_ref[...])
    for pair in range(width // 128):
        cut = slice(pair * 128, (pair + 1) * 128)
        first, second = 2 * pair, 2 * pair + 1
        x_own = x_ref[:, cut]
        column = jnp.where(low, col_part[:, first : first + 1], col_part[:, second : second + 1])
        row = jnp.where(low, row_part[first : first + 1], row_part[second : second + 1])
        step = jnp.where(low, steps_twice[first : first + 1], steps_twice[second : second + 1])
        kernel = jnp.exp(jnp.minimum(column + row, 0.0)) * scores * step
        high = kernel.astype(BF16)
        rest = (kernel - high.astype(F32)).astype(BF16)
        none = jnp.zeros_like(x_own)
        values = jnp.concatenate(
            [jnp.where(low, x_own, none), zeros, jnp.where(low, none, x_own), zeros], axis=0
        )
        mixed = jnp.dot(jnp.concatenate([high, rest], axis=0), values, preferred_element_type=F32)
        skip = jnp.where(low, skips[first : first + 1], skips[second : second + 1])
        mixed_ref[:, cut] = mixed[:rows] + mixed[rows:] + skip * x_own.astype(F32)
        gate = raw_gate_ref[:, cut].astype(F32)
        gate_ref[:, cut] = gate / (1.0 + jnp.exp(-gate))
        decay_ref[:, cut] = jnp.exp(column)


def mixer_kernel(
    mixed_ref, gate_ref, decay_ref, res_ref, c_ref, rate_ref, gain_ref, x_ref, b_ref, step_ref, out_ref
):
    rows, width = x_ref.shape
    heads = step_ref.shape[0]
    size = width // heads
    steps = softplus(step_ref[...])
    decay = steps * -jnp.exp(as_column(rate_ref[...]))
    down, across = iotas(rows, rows)
    after = jnp.where(down > across, 1.0, 0.0)
    same = jnp.where(down == across, 1.0, 0.0)
    carried = jnp.exp(jnp.dot(decay, after, precision=EXACT, preferred_element_type=F32)) * steps
    carried = lax.dot_general(same, carried, LAST, precision=EXACT, preferred_element_type=F32)
    scores = lax.dot_general(c_ref[...], b_ref[...], LAST, preferred_element_type=F32)
    s_high = scores.astype(BF16)
    s_rest = (scores - s_high.astype(F32)).astype(BF16)
    s_both = jnp.concatenate([s_high, s_rest], axis=0)
    low = lax.broadcasted_iota(jnp.int32, (1, 128), 1) < size
    for pair in range(width // 128):
        cut = slice(pair * 128, (pair + 1) * 128)
        first, second = 2 * pair, 2 * pair + 1
        weight = jnp.where(low, carried[:, first : first + 1], carried[:, second : second + 1])
        values = weight * x_ref[:, cut].astype(F32)
        v_high = values.astype(BF16)
        v_rest = (values - v_high.astype(F32)).astype(BF16)
        cross = jnp.dot(s_both, v_high, preferred_element_type=F32)
        cross = cross[:rows] + cross[rows:] + jnp.dot(s_high, v_rest, preferred_element_type=F32)
        gated = (mixed_ref[:, cut] + decay_ref[:, cut] * cross) * gate_ref[:, cut]
        square = gated * gated
        mean_low = jnp.sum(jnp.where(low, square, 0.0), axis=1, keepdims=True) / size
        mean_high = jnp.sum(jnp.where(low, 0.0, square), axis=1, keepdims=True) / size
        scale = lax.rsqrt(jnp.where(low, mean_low, mean_high) + EPSILON)
        normed = gated * scale * gain_ref[:, cut]
        out_ref[:, cut] = (res_ref[:, cut].astype(F32) + normed).astype(BF16)


def add_up(blocks, gain, weights, scaled):
    rows, width = blocks[0].shape
    squares = []
    for i, block in enumerate(blocks):
        wide = block[...].astype(F32)
        squares.append(jnp.sum(wide * wide, axis=1, keepdims=True))
        scaled[i * rows : (i + 1) * rows] = (wide * gain).astype(BF16)
    return jnp.dot(scaled[...], weights, preferred_element_type=F32), jnp.concatenate(squares, axis=0)


def first_up_kernel(expert, count, *refs):
    blocks, (up_hbm, down_hbm, gain_hbm, ids_hbm, weight_hbm) = refs[:count], refs[count : count + 5]
    total_ref, square_ref, up_ref, down_ref, gain_ref, route_ref = refs[count + 5 : count + 11]
    tiles, gains, ids, weights, scaled, sems = refs[count + 11 :]
    me = lax.axis_index(expert)
    width = tiles.shape[1]
    pairs = []
    for k in range(2):
        pairs.append((gain_hbm.at[:, pl.ds(pl.multiple_of((me ^ k) * width, width), width)], gains.at[k]))
    for k in range(2):
        pairs.append((up_hbm.at[pl.ds(pl.multiple_of((me ^ k) * width, width), width)], tiles.at[k]))
    for k in range(2):
        start = pl.multiple_of((me ^ (k + 2)) * width, width)
        pairs.append((gain_hbm.at[:, pl.ds(start, width)], gain_ref.at[k]))
        pairs.append((up_hbm.at[pl.ds(start, width)], up_ref.at[k]))
    pairs += [(ids_hbm, ids), (weight_hbm, weights), (down_hbm, down_ref)]
    copies = fetch(pairs, sems)
    total, squares = None, None
    for k in range(2):
        copies[k].wait()
        copies[2 + k].wait()
        part, square = add_up(
            [b.at[:, k * width : (k + 1) * width] for b in blocks], gains[k], tiles[k], scaled
        )
        total = part if total is None else total + part
        squares = square if squares is None else squares + square
    total_ref[...] = total
    square_ref[...] = squares
    for copy in copies[4:]:
        copy.wait()
    row = jnp.sum(jnp.where(ids[...] == me, weights[...], 0.0), axis=0, keepdims=True)
    route_ref[...] = as_column(row)


def second_up_kernel(count, model, *refs):
    blocks, (total_ref, square_ref, up_ref, gain_ref) = refs[:count], refs[count : count + 4]
    out_ref, scaled = refs[count + 4 :]
    width = up_ref.shape[1]
    total, squares = total_ref[...], square_ref[...]
    for k in range(2):
        part, square = add_up(
            [b.at[:, k * width : (k + 1) * width] for b in blocks], gain_ref[k], up_ref[k], scaled
        )
        total += part
        squares += square
    value = total * lax.rsqrt(squares / model + EPSILON)
    out_ref[...] = (value / (1.0 + jnp.exp(-value))).astype(BF16)


def down_kernel(rows, columns, act_ref, down_ref, out_ref):
    out_ref[...] = jnp.dot(
        act_ref[rows], down_ref[:, columns], preferred_element_type=F32
    ).astype(BF16)


def add_kernel(own_ref, other_ref, *outs):
    rows = outs[0].shape[0]
    for i, out in enumerate(outs):
        cut = slice(i * rows, (i + 1) * rows)
        out[...] = (own_ref[cut].astype(F32) + other_ref[cut].astype(F32)).astype(BF16)


def weigh_kernel(expert, own_ref, *refs):
    others, route_ref, outs = refs[:3], refs[3], refs[4:]
    me = lax.axis_index(expert)
    rows = own_ref.shape[0]
    keep = outs[0].shape[0]
    total = own_ref[...].astype(F32)
    for other in others:
        total += other[...].astype(F32)
    total = (total * route_ref[...]).astype(BF16)
    place, source = iotas(16 * len(outs), rows)
    wanted = ((place // 16) ^ me) * keep + place % 16
    pick = jnp.where((place % 16 < keep) & (source == wanted), 1.0, 0.0).astype(BF16)
    picked = jnp.dot(pick, total, preferred_element_type=F32)
    for k, out in enumerate(outs):
        out[...] = picked[16 * k : 16 * k + keep].astype(BF16)


def call(kernel, outs, inputs, name, scratch=(), in_hbm=(), limit=16):
    vmem, hbm = pl.BlockSpec(memory_space=pltpu.VMEM), pl.BlockSpec(memory_space=pl.ANY)
    return pl.pallas_call(
        kernel,
        out_shape=[jax.ShapeDtypeStruct(shape, dtype) for shape, dtype in outs],
        in_specs=[hbm if i in in_hbm else vmem for i in range(len(inputs))],
        out_specs=[vmem] * len(outs),
        scratch_shapes=scratch,
        compiler_params=pltpu.CompilerParams(vmem_limit_bytes=limit * MIB),
        name=name,
    )(*inputs)


def plane_body(
    residual, ssm_input, ssm_gate, input_map, output_map, step_raw, log_rate, skip_gain, head_gain,
    moe_gain, expert_ids, gate_weight, expert_up, expert_down,
):
    rows, width = residual.shape[1:]
    heads = log_rate.shape[0]
    state = input_map.shape[2]
    experts = lax.axis_size("exp")
    model = experts * width
    units = expert_up.shape[2]
    plane = ("dp", "ctx")

    def along_z(block, k):
        return lax.ppermute(block, "exp", [(i, i ^ k) for i in range(experts)])

    def in_plane(block, x, y, core):
        route = [
            (d * 2 + c, (d ^ (y * 2) ^ core) * 2 + (c ^ x)) for d in range(4) for c in range(2)
        ]
        return lax.ppermute(block, plane, route)

    step_t = step_raw[0].T
    before = [lax.ppermute(a, "ctx", [(0, 1)]) for a in (ssm_input[0], input_map[0], step_t)]
    wide, flat = (rows, width), (rows, state)
    own = call(
        own_kernel,
        [(wide, F32), (wide, F32), (wide, F32), (wide, BF16), (flat, BF16), ((1, heads), F32), ((1, width), F32)],
        [
            ssm_input[0], ssm_gate[0], residual[0], input_map[0], output_map[0], step_t,
            log_rate[None], head_gain[None], skip_gain[None],
        ],
        "mixer_own",
        scratch=[
            pltpu.VMEM(wide, BF16), pltpu.VMEM(wide, BF16), pltpu.VMEM(flat, BF16),
            pltpu.VMEM((heads, rows), F32), pltpu.VMEM((1, heads), F32), pltpu.SemaphoreType.DMA((9,)),
        ],
        in_hbm=range(9),
    )
    (hidden,) = call(mixer_kernel, [(wide, BF16)], [*own, *before], "mixer")
    chips = ((0, 0), (1, 0), (0, 1), (1, 1))

    def gathered(block):
        mine = [block] + [in_plane(block, x, y, 0) for x, y in chips[1:]]
        return mine + [in_plane(b, 0, 0, 1) for b in mine]

    near = along_z(hidden, 1)
    far = [along_z(hidden, 2), along_z(hidden, 3)]
    first = gathered(jnp.concatenate([hidden, near], axis=1))
    second = gathered(jnp.concatenate(far, axis=1))
    blocks = len(first)
    count = blocks * rows
    total, squares, up_rest, down, gain_rest, route = call(
        functools.partial(first_up_kernel, "exp", blocks),
        [
            ((count, units), F32), ((count, 1), F32), ((2, width, units), BF16), ((units, model), BF16),
            ((2, 1, width), F32), ((rows, 1), F32),
        ],
        [*first, expert_up[0], expert_down[0], moe_gain[None], expert_ids[0].T, gate_weight[0].T],
        "up_first",
        scratch=[
            pltpu.VMEM((2, width, units), BF16), pltpu.VMEM((2, 1, width), F32),
            pltpu.VMEM((2, rows), jnp.int32), pltpu.VMEM((2, rows), F32),
            pltpu.VMEM((count, width), BF16), pltpu.SemaphoreType.DMA((11,)),
        ],
        in_hbm=range(blocks, blocks + 5),
        limit=32,
    )
    (activated,) = call(
        functools.partial(second_up_kernel, blocks, model),
        [((count, units), BF16)],
        [*second, total, squares, up_rest, gain_rest],
        "up_second",
        scratch=[pltpu.VMEM((count, width), BF16)],
        limit=24,
    )
    keep = rows // experts
    ends = []
    for low, high in ((0, model // 2), (model // 2, model)):
        cut = high - low
        sibling, mine = [
            call(
                functools.partial(down_kernel, slice(a, a + count // 2), slice(low, high)),
                [((count // 2, cut), BF16)],
                [activated, down],
                "down",
            )[0]
            for a in (count // 2, 0)
        ]
        summed = call(
            add_kernel, [((rows, cut), BF16)] * 4, [mine, in_plane(sibling, 0, 0, 1)], "add_cores"
        )
        returned = [in_plane(summed[i], x, y, 0) for i, (x, y) in enumerate(chips) if i]
        slices = call(
            functools.partial(weigh_kernel, "exp"),
            [((keep, cut), BF16)] * experts,
            [summed[0], *returned, route],
            "weigh",
        )
        final = slices[0].astype(F32)
        for k in range(1, experts):
            final += along_z(slices[k], k).astype(F32)
        ends.append(final.astype(BF16))
    return (hidden[None], jnp.concatenate(ends, axis=1)[None])


def solution(mesh):
    placed = (
        P("dp", "ctx", "exp"),
        P("dp", "ctx", "exp"),
        P("dp", "ctx", "exp"),
        P("dp", "ctx", None),
        P("dp", "ctx", None),
        P("dp", "ctx", "exp"),
        P("exp"),
        P("exp"),
        P("exp"),
        P(),
        P("dp", "ctx", None),
        P("dp", "ctx", None),
        P("exp", None, ("dp", "ctx")),
        P("exp", ("dp", "ctx"), None),
    )
    sizes = tuple(mesh.shape[axis] for axis in ("dp", "ctx", "exp"))
    return jax.shard_map(
        plane_body if sizes == (4, 2, 4) else body,
        mesh=mesh,
        in_specs=placed,
        out_specs=(P("dp", "ctx", "exp"), P("dp", ("ctx", "exp"), None)),
        check_vma=False,
    )
```

```python
import functools

import jax
import jax.numpy as jnp
from jax import lax
from jax.experimental import pallas as pl
from jax.experimental.pallas import tpu as pltpu
from jax.sharding import PartitionSpec as P

EPSILON = 1e-05
BF16 = jnp.bfloat16
F32 = jnp.float32
MIB = 1 << 20
EXACT = lax.Precision.HIGHEST
LAST = (((1,), (1,)), ((), ()))


def shifted(block, axis, distance):
    devices = range(lax.axis_size(axis))
    route = [(i - distance, i) for i in devices if i - distance in devices]
    return lax.ppermute(block, axis, route)


def route_slots(routes, experts):
    blocks = routes.shape[0]
    ordered = routes.reshape(blocks, -1)
    matches = (ordered[:, :, None] == jnp.arange(experts, dtype=jnp.int32)[None, None, :]).astype(
        jnp.int32
    )
    earlier = jnp.cumsum(matches, axis=1) - matches
    return jnp.sum(earlier * matches, axis=2).reshape(routes.shape)


def body(
    residual,
    ssm_input,
    ssm_gate,
    input_map,
    output_map,
    step_raw,
    log_rate,
    skip_gain,
    head_gain,
    moe_gain,
    expert_ids,
    gate_weight,
    expert_up,
    expert_down,
):
    heads_loc = log_rate.shape[0]
    local_rows = residual.shape[1]
    width_loc = residual.shape[2]
    head_size = width_loc // heads_loc
    values = ssm_input[0].astype(jnp.float32).reshape(local_rows, heads_loc, head_size)
    step_size = jax.nn.softplus(step_raw[0])
    cumulative = jnp.cumsum(step_size * (-jnp.exp(log_rate))[None, :], axis=0)
    scores = jnp.einsum(
        "tn,sn->ts", output_map[0], input_map[0], preferred_element_type=jnp.float32
    )
    positions = jnp.arange(local_rows)
    causal = positions[:, None] >= positions[None, :]
    spread = cumulative[:, None, :] - cumulative[None, :, :]
    kernel = (
        jnp.where(causal[:, :, None], jnp.exp(jnp.minimum(spread, 0.0)), 0.0)
        * scores[:, :, None]
        * step_size[None, :, :]
    )
    within = jnp.einsum("tsh,shp->thp", kernel, values, precision=lax.Precision.HIGHEST)
    ending = cumulative[-1]
    carried = jnp.exp(ending[None, :] - cumulative) * step_size
    in_map_wide = input_map[0].astype(jnp.float32)
    out_map_wide = output_map[0].astype(jnp.float32)
    local_state = jnp.einsum(
        "sh,shp,sn->hpn", carried, values, in_map_wide, precision=lax.Precision.HIGHEST
    )
    total_decay = jnp.exp(ending)
    incoming = jnp.zeros_like(local_state)
    for repeat in range(lax.axis_size("ctx") - 1):
        outgoing = total_decay[:, None, None] * incoming + local_state
        incoming = shifted(outgoing.astype(jnp.bfloat16), "ctx", 1).astype(outgoing.dtype)
    across_heads = (
        jnp.einsum("tn,hpn->thp", out_map_wide, incoming, precision=lax.Precision.HIGHEST)
        * jnp.exp(cumulative)[:, :, None]
    )
    mixed_y = within + across_heads + skip_gain[None, :, None] * values
    gated = mixed_y * jax.nn.silu(
        ssm_gate[0].astype(jnp.float32).reshape(local_rows, heads_loc, head_size)
    )
    normed = (
        gated
        * lax.rsqrt(jnp.mean(gated * gated, axis=2, keepdims=True) + EPSILON)
        * head_gain.reshape(heads_loc, head_size)
    )
    hidden = (residual[0].astype(jnp.float32) + normed.reshape(local_rows, width_loc)).astype(
        jnp.bfloat16
    )
    exp_count = lax.axis_size("exp")
    my_expert = lax.axis_index("exp")
    tok_rows = local_rows // exp_count
    capacity = min(tok_rows, max(4, 4 * tok_rows // exp_count))
    model_width = width_loc * exp_count
    routes_all = expert_ids[0].reshape(exp_count, tok_rows, 2)
    slots_all = route_slots(routes_all, exp_count)
    targets_all = routes_all * capacity + slots_all
    slot_ids = jnp.arange(exp_count * capacity, dtype=jnp.int32)
    own_targets = lax.dynamic_slice_in_dim(targets_all, my_expert, 1, 0)[0]
    own_weights = lax.dynamic_slice_in_dim(
        gate_weight[0].reshape(exp_count, tok_rows, 2), my_expert, 1, 0
    )[0]
    hidden_wide = hidden.astype(jnp.float32)
    squared_values = lax.psum(jnp.sum(hidden_wide * hidden_wide, axis=1), "exp")
    gain_part = lax.dynamic_slice_in_dim(moe_gain, my_expert * width_loc, width_loc, 0)
    normal_part = (
        hidden_wide
        * lax.rsqrt(squared_values[:, None] / model_width + EPSILON)
        * gain_part[None, :]
    ).astype(jnp.bfloat16)
    placing_all = jnp.any(
        slot_ids[None, :, None, None] == targets_all[:, None, :, :], axis=3
    ).astype(jnp.bfloat16)
    outbound = jnp.einsum(
        "bqt,btc->bqc",
        placing_all,
        normal_part.reshape(exp_count, tok_rows, width_loc),
        preferred_element_type=jnp.float32,
    )
    outbound = outbound.astype(jnp.bfloat16).reshape(exp_count, exp_count, capacity, width_loc)
    arrived = lax.all_to_all(outbound, "exp", split_axis=1, concat_axis=3, tiled=True).reshape(
        exp_count * capacity, model_width
    )
    up_local = expert_up[0]
    down_local = expert_down[0]
    activated = jax.nn.silu(
        jnp.dot(
            lax.all_gather(arrived, ("dp", "ctx"), axis=0, tiled=True),
            up_local,
            preferred_element_type=jnp.float32,
        )
    ).astype(jnp.bfloat16)
    summed = lax.psum_scatter(
        jnp.dot(activated, down_local, preferred_element_type=jnp.float32).astype(jnp.bfloat16),
        ("dp", "ctx"),
        scatter_dimension=0,
        tiled=True,
    )
    sent_back = summed.reshape(exp_count, capacity, model_width)
    returned = lax.all_to_all(sent_back, "exp", split_axis=0, concat_axis=0, tiled=True).reshape(
        exp_count * capacity, model_width
    )
    picking = (own_targets.reshape(-1)[:, None] == slot_ids[None, :]).astype(jnp.bfloat16)
    chosen = jnp.dot(picking, returned, preferred_element_type=jnp.float32).reshape(
        tok_rows, 2, model_width
    )
    combined = jnp.sum(own_weights[:, :, None] * chosen, axis=1).astype(jnp.bfloat16)
    return (hidden[None], combined[None])


def softplus(raw):
    return jnp.maximum(raw, 0.0) + jnp.log1p(jnp.exp(-jnp.abs(raw)))


def iotas(rows, columns):
    shape = (rows, columns)
    return lax.broadcasted_iota(jnp.int32, shape, 0), lax.broadcasted_iota(jnp.int32, shape, 1)


def as_column(row):
    size = row.shape[1]
    down, across = iotas(size, size)
    return jnp.sum(jnp.where(down == across, row, 0.0), axis=1, keepdims=True)


def fetch(pairs, sems):
    copies = [pltpu.make_async_copy(a, b, sems.at[i]) for i, (a, b) in enumerate(pairs)]
    for copy in copies:
        copy.start()
    return copies


def own_kernel(
    x_hbm, gate_hbm, res_hbm, b_hbm, c_hbm, step_hbm, rate_hbm, gain_hbm, skip_hbm,
    mixed_ref, gate_ref, decay_ref, res_ref, c_ref, rate_ref, gain_ref,
    x_ref, raw_gate_ref, b_ref, step_ref, skip_ref, sems,
):
    copies = fetch(
        [
            (step_hbm, step_ref), (rate_hbm, rate_ref), (b_hbm, b_ref), (c_hbm, c_ref), (x_hbm, x_ref),
            (skip_hbm, skip_ref), (gate_hbm, raw_gate_ref), (res_hbm, res_ref), (gain_hbm, gain_ref),
        ],
        sems,
    )
    rows, width = x_ref.shape
    heads = step_ref.shape[0]
    size = width // heads
    pad = 64 - rows
    copies[0].wait()
    copies[1].wait()
    steps = softplus(step_ref[...])
    decay = steps * -jnp.exp(as_column(rate_ref[...]))
    down, across = iotas(rows, 128)
    place = across & 63
    to_row = jnp.where((down <= place) & (place < rows), -1.0, 0.0)
    to_step = jnp.where(down == place, 1.0, 0.0)
    row_part = jnp.dot(decay, to_row, precision=EXACT, preferred_element_type=F32)
    steps_twice = jnp.dot(steps, to_step, precision=EXACT, preferred_element_type=F32)
    t_row, u_col = iotas(rows, rows)
    to_col = jnp.where(u_col <= t_row, 1.0, 0.0)
    col_part = lax.dot_general(to_col, decay, LAST, precision=EXACT, preferred_element_type=F32)
    copies[2].wait()
    copies[3].wait()
    zeros = jnp.zeros((pad, b_ref.shape[1]), BF16)
    maps = jnp.concatenate([b_ref[...], zeros, b_ref[...], zeros], axis=0)
    scores = lax.dot_general(c_ref[...], maps, LAST, preferred_element_type=F32)
    scores = jnp.where(place <= down, scores, 0.0)
    lane = lax.broadcasted_iota(jnp.int32, (1, 128), 1)
    low = lane < size
    zeros = jnp.zeros((pad, 128), BF16)
    for copy in copies[4:]:
        copy.wait()
    skips = as_column(skip_ref[...])
    for pair in range(width // 128):
        cut = slice(pair * 128, (pair + 1) * 128)
        first, second = 2 * pair, 2 * pair + 1
        x_own = x_ref[:, cut]
        column = jnp.where(low, col_part[:, first : first + 1], col_part[:, second : second + 1])
        row = jnp.where(low, row_part[first : first + 1], row_part[second : second + 1])
        step = jnp.where(low, steps_twice[first : first + 1], steps_twice[second : second + 1])
        kernel = jnp.exp(jnp.minimum(column + row, 0.0)) * scores * step
        high = kernel.astype(BF16)
        rest = (kernel - high.astype(F32)).astype(BF16)
        none = jnp.zeros_like(x_own)
        values = jnp.concatenate(
            [jnp.where(low, x_own, none), zeros, jnp.where(low, none, x_own), zeros], axis=0
        )
        mixed = jnp.dot(jnp.concatenate([high, rest], axis=0), values, preferred_element_type=F32)
        skip = jnp.where(low, skips[first : first + 1], skips[second : second + 1])
        mixed_ref[:, cut] = mixed[:rows] + mixed[rows:] + skip * x_own.astype(F32)
        gate = raw_gate_ref[:, cut].astype(F32)
        gate_ref[:, cut] = gate / (1.0 + jnp.exp(-gate))
        decay_ref[:, cut] = jnp.exp(column)


def mixer_kernel(
    mixed_ref, gate_ref, decay_ref, res_ref, c_ref, rate_ref, gain_ref, x_ref, b_ref, step_ref, out_ref, copy_ref
):
    rows, width = x_ref.shape
    heads = step_ref.shape[0]
    size = width // heads
    steps = softplus(step_ref[...])
    decay = steps * -jnp.exp(as_column(rate_ref[...]))
    down, across = iotas(rows, rows)
    after = jnp.where(down > across, 1.0, 0.0)
    same = jnp.where(down == across, 1.0, 0.0)
    carried = jnp.exp(jnp.dot(decay, after, precision=EXACT, preferred_element_type=F32)) * steps
    carried = lax.dot_general(same, carried, LAST, precision=EXACT, preferred_element_type=F32)
    scores = lax.dot_general(c_ref[...], b_ref[...], LAST, preferred_element_type=F32)
    s_high = scores.astype(BF16)
    s_rest = (scores - s_high.astype(F32)).astype(BF16)
    s_both = jnp.concatenate([s_high, s_rest], axis=0)
    low = lax.broadcasted_iota(jnp.int32, (1, 128), 1) < size
    for pair in range(width // 128):
        cut = slice(pair * 128, (pair + 1) * 128)
        first, second = 2 * pair, 2 * pair + 1
        weight = jnp.where(low, carried[:, first : first + 1], carried[:, second : second + 1])
        values = weight * x_ref[:, cut].astype(F32)
        v_high = values.astype(BF16)
        v_rest = (values - v_high.astype(F32)).astype(BF16)
        cross = jnp.dot(s_both, v_high, preferred_element_type=F32)
        cross = cross[:rows] + cross[rows:] + jnp.dot(s_high, v_rest, preferred_element_type=F32)
        gated = (mixed_ref[:, cut] + decay_ref[:, cut] * cross) * gate_ref[:, cut]
        square = gated * gated
        mean_low = jnp.sum(jnp.where(low, square, 0.0), axis=1, keepdims=True) / size
        mean_high = jnp.sum(jnp.where(low, 0.0, square), axis=1, keepdims=True) / size
        scale = lax.rsqrt(jnp.where(low, mean_low, mean_high) + EPSILON)
        normed = gated * scale * gain_ref[:, cut]
        hidden = (res_ref[:, cut].astype(F32) + normed).astype(BF16)
        out_ref[:, cut] = hidden
        copy_ref[:, cut] = hidden


def add_up(blocks, gain, weights, scaled):
    rows, width = blocks[0].shape
    squares = []
    for i, block in enumerate(blocks):
        wide = block[...].astype(F32)
        squares.append(jnp.sum(wide * wide, axis=1, keepdims=True))
        scaled[i * rows : (i + 1) * rows] = (wide * gain).astype(BF16)
    return jnp.dot(scaled[...], weights, preferred_element_type=F32), jnp.concatenate(squares, axis=0)


def load_kernel(expert, up_hbm, gain_hbm, up_ref, gain_ref, sems):
    me = lax.axis_index(expert)
    slices, width = up_ref.shape[:2]
    pairs = []
    for k in range(slices):
        cut = pl.ds(pl.multiple_of((me ^ k) * width, width), width)
        pairs += [(up_hbm.at[cut], up_ref.at[k]), (gain_hbm.at[:, cut], gain_ref.at[k])]
    for copy in fetch(pairs, sems):
        copy.wait()


def first_up_kernel(expert, count, *refs):
    blocks, (up_ref, gain_ref, down_hbm, ids_hbm, weight_hbm) = refs[:count], refs[count : count + 5]
    total_ref, square_ref, down_ref, route_ref = refs[count + 5 : count + 9]
    ids, weights, scaled, sems = refs[count + 9 :]
    copies = fetch([(down_hbm, down_ref), (ids_hbm, ids), (weight_hbm, weights)], sems)
    total_ref[...], square_ref[...] = add_up(blocks, gain_ref[0], up_ref[0], scaled)
    for copy in copies:
        copy.wait()
    row = jnp.sum(
        jnp.where(ids[...] == lax.axis_index(expert), weights[...], 0.0), axis=0, keepdims=True
    )
    route_ref[...] = as_column(row)


def second_up_kernel(count, rows, model, *refs):
    blocks, (total_ref, square_ref, up_ref, gain_ref, out_ref, scaled) = refs[:count], refs[count:]
    slices, width = up_ref.shape[:2]
    total, squares = total_ref[rows], square_ref[rows]
    for k in range(1, slices):
        cut = slice((k - 1) * width, k * width)
        part, square = add_up([b.at[:, cut] for b in blocks], gain_ref[k], up_ref[k], scaled)
        total += part
        squares += square
    value = total * lax.rsqrt(squares / model + EPSILON)
    out_ref[...] = (value / (1.0 + jnp.exp(-value))).astype(BF16)


def down_kernel(columns, act_ref, down_ref, out_ref):
    out_ref[...] = jnp.dot(
        act_ref[...], down_ref[:, columns], preferred_element_type=F32
    ).astype(BF16)


def join_kernel(*refs):
    blocks, out_ref = refs[:-1], refs[-1]
    width = blocks[0].shape[1]
    for i, block in enumerate(blocks):
        out_ref[:, i * width : (i + 1) * width] = block[...]


def stack_kernel(*refs):
    blocks, out_ref = refs[:-1], refs[-1]
    rows = blocks[0].shape[0]
    for i, block in enumerate(blocks):
        out_ref[i * rows : (i + 1) * rows] = block[...]


def add_kernel(own_ref, other_ref, *outs):
    rows = outs[0].shape[0]
    for i, out in enumerate(outs):
        cut = slice(i * rows, (i + 1) * rows)
        out[...] = (own_ref[cut].astype(F32) + other_ref[cut].astype(F32)).astype(BF16)


def weigh_kernel(expert, own_ref, *refs):
    others, route_ref, outs = refs[:3], refs[3], refs[4:]
    me = lax.axis_index(expert)
    rows = own_ref.shape[0]
    keep = outs[0].shape[0]
    total = own_ref[...].astype(F32)
    for other in others:
        total += other[...].astype(F32)
    total = (total * route_ref[...]).astype(BF16)
    place, source = iotas(16 * len(outs), rows)
    wanted = ((place // 16) ^ me) * keep + place % 16
    pick = jnp.where((place % 16 < keep) & (source == wanted), 1.0, 0.0).astype(BF16)
    picked = jnp.dot(pick, total, preferred_element_type=F32)
    for k, out in enumerate(outs):
        out[...] = picked[16 * k : 16 * k + keep].astype(BF16)


def call(kernel, outs, inputs, name, scratch=(), in_hbm=(), limit=16, us=0.01, after=()):
    vmem, hbm = pl.BlockSpec(memory_space=pltpu.VMEM), pl.BlockSpec(memory_space=pltpu.HBM)
    inputs = [
        pltpu.with_memory_space_constraint(a, pltpu.HBM) if i in in_hbm else a for i, a in enumerate(inputs)
    ]
    given, extra = len(inputs), len(after)

    def without(*refs):
        return kernel(*refs[:given], *refs[given + extra :])

    return pl.pallas_call(
        without,
        out_shape=[jax.ShapeDtypeStruct(shape, dtype) for shape, dtype in outs],
        in_specs=[hbm if i in in_hbm else vmem for i in range(given)]
        + [pl.BlockSpec(memory_space=pl.ANY)] * extra,
        out_specs=[vmem] * len(outs),
        scratch_shapes=scratch,
        compiler_params=pltpu.CompilerParams(vmem_limit_bytes=limit * MIB),
        cost_estimate=pl.CostEstimate(
            flops=int(us * 1e9), bytes_accessed=int(us * 3e6), transcendentals=0
        ),
        name=name,
    )(*inputs, *after)


def plane_body(
    residual, ssm_input, ssm_gate, input_map, output_map, step_raw, log_rate, skip_gain, head_gain,
    moe_gain, expert_ids, gate_weight, expert_up, expert_down,
):
    rows, width = residual.shape[1:]
    heads = log_rate.shape[0]
    state = input_map.shape[2]
    experts = lax.axis_size("exp")
    model = experts * width
    units = expert_up.shape[2]
    plane = ("dp", "ctx")

    def along_z(block, k):
        return lax.ppermute(block, "exp", [(i, i ^ k) for i in range(experts)])

    def in_plane(block, x, y, core):
        route = [
            (d * 2 + c, (d ^ (y * 2) ^ core) * 2 + (c ^ x)) for d in range(4) for c in range(2)
        ]
        return lax.ppermute(block, plane, route)

    step_t = step_raw[0].T
    before = [lax.ppermute(a, "ctx", [(0, 1)]) for a in (ssm_input[0], input_map[0], step_t)]
    wide, flat = (rows, width), (rows, state)
    own = call(
        own_kernel,
        [(wide, F32), (wide, F32), (wide, F32), (wide, BF16), (flat, BF16), ((1, heads), F32), ((1, width), F32)],
        [
            ssm_input[0], ssm_gate[0], residual[0], input_map[0], output_map[0], step_t,
            log_rate[None], head_gain[None], skip_gain[None],
        ],
        "mixer_own",
        scratch=[
            pltpu.VMEM(wide, BF16), pltpu.VMEM(wide, BF16), pltpu.VMEM(flat, BF16),
            pltpu.VMEM((heads, rows), F32), pltpu.VMEM((1, heads), F32), pltpu.SemaphoreType.DMA((9,)),
        ],
        in_hbm=range(9),
    )
    hidden, sent = call(mixer_kernel, [(wide, BF16), (wide, BF16)], [*own, *before], "mixer")
    chips = ((0, 0), (1, 0), (0, 1), (1, 1))

    def joined(blocks, name, after=(), us=0.01):
        shape = (rows, width * len(blocks))
        return call(join_kernel, [(shape, BF16)], blocks, name, after=after, us=us)[0]

    arrived_z = [along_z(sent, k) for k in range(1, experts)]
    near = [sent] + [in_plane(sent, x, y, 0) for x, y in chips[1:]]
    corner = [along_z(near[3], k) for k in range(1, experts)]
    up, gain = call(
        functools.partial(load_kernel, "exp"),
        [((experts, width, units), BF16), ((experts, 1, width), F32)],
        [expert_up[0], moe_gain[None]],
        "load_up",
        scratch=[pltpu.SemaphoreType.DMA((2 * experts,))],
        in_hbm=range(2),
        after=near[3:],
    )
    rest = joined(arrived_z, "join_z")
    second = [rest] + [in_plane(rest, x, y, 0) for x, y in chips[1:3]]
    (first,) = call(
        stack_kernel, [((rows * len(near), width), BF16)], near, "stack_first", after=[rest]
    )
    first = [first, in_plane(first, 0, 0, 1)]
    half = first[0].shape[0]
    count = 2 * half
    total, squares, down, route = call(
        functools.partial(first_up_kernel, "exp", 2),
        [((count, units), F32), ((count, 1), F32), ((units, model), BF16), ((rows, 1), F32)],
        [*first, up, gain, expert_down[0], expert_ids[0].T, gate_weight[0].T],
        "up_first",
        scratch=[
            pltpu.VMEM((2, rows), jnp.int32), pltpu.VMEM((2, rows), F32),
            pltpu.VMEM((count, width), BF16), pltpu.SemaphoreType.DMA((3,)),
        ],
        in_hbm=range(4, 7),
        limit=32,
    )
    *others, total = lax.optimization_barrier((*second[1:], *corner, total))
    second = [rest, *others[:2], joined(others[2:], "join_corner", us=10.0)]
    activated = []
    for i, blocks in enumerate((second, [in_plane(block, 0, 0, 1) for block in second])):
        activated += call(
            functools.partial(second_up_kernel, len(blocks), slice(i * half, (i + 1) * half), model),
            [((half, units), BF16)],
            [*blocks, total, squares, up, gain],
            "up_second",
            scratch=[pltpu.VMEM((half, width), BF16)],
            limit=24,
            after=activated,
        )
    keep = rows // experts
    ends, before_this = [], []
    middle = model // 2
    cuts = ((0, middle), (middle, model))

    def down_part(i, low, high, after):
        return call(
            functools.partial(down_kernel, slice(low, high)),
            [((half, high - low), BF16)],
            [activated[i], down],
            "down",
            after=after,
        )

    for low, high in cuts:
        cut = high - low
        (sibling,) = down_part(1, low, high, before_this)
        (mine,) = down_part(0, low, high, [sibling])
        summed = call(
            add_kernel, [((rows, cut), BF16)] * 4, [mine, in_plane(sibling, 0, 0, 1)], "add_cores"
        )
        before_this = summed[:1]
        returned = [in_plane(summed[i], x, y, 0) for i, (x, y) in enumerate(chips) if i]
        slices = call(
            functools.partial(weigh_kernel, "exp"),
            [((keep, cut), BF16)] * experts,
            [summed[0], *returned, route],
            "weigh",
        )
        final = slices[0].astype(F32)
        for k in range(1, experts):
            final += along_z(slices[k], k).astype(F32)
        ends.append(final.astype(BF16))
    return (hidden[None], jnp.concatenate(ends, axis=1)[None])


def solution(mesh):
    placed = (
        P("dp", "ctx", "exp"),
        P("dp", "ctx", "exp"),
        P("dp", "ctx", "exp"),
        P("dp", "ctx", None),
        P("dp", "ctx", None),
        P("dp", "ctx", "exp"),
        P("exp"),
        P("exp"),
        P("exp"),
        P(),
        P("dp", "ctx", None),
        P("dp", "ctx", None),
        P("exp", None, ("dp", "ctx")),
        P("exp", ("dp", "ctx"), None),
    )
    sizes = tuple(mesh.shape[axis] for axis in ("dp", "ctx", "exp"))
    return jax.shard_map(
        plane_body if sizes == (4, 2, 4) else body,
        mesh=mesh,
        in_specs=placed,
        out_specs=(P("dp", "ctx", "exp"), P("dp", ("ctx", "exp"), None)),
        check_vma=False,
    )
```

```python
import functools

import jax
import jax.numpy as jnp
from jax import lax
from jax.experimental import pallas as pl
from jax.experimental.pallas import tpu as pltpu
from jax.sharding import PartitionSpec as P

EPSILON = 1e-05
BF16 = jnp.bfloat16
CORNER = (1, 2)
JOIN = 10.0
F32 = jnp.float32
MIB = 1 << 20
EXACT = lax.Precision.HIGHEST
LAST = (((1,), (1,)), ((), ()))


def shifted(block, axis, distance):
    devices = range(lax.axis_size(axis))
    route = [(i - distance, i) for i in devices if i - distance in devices]
    return lax.ppermute(block, axis, route)


def route_slots(routes, experts):
    blocks = routes.shape[0]
    ordered = routes.reshape(blocks, -1)
    matches = (ordered[:, :, None] == jnp.arange(experts, dtype=jnp.int32)[None, None, :]).astype(
        jnp.int32
    )
    earlier = jnp.cumsum(matches, axis=1) - matches
    return jnp.sum(earlier * matches, axis=2).reshape(routes.shape)


def body(
    residual,
    ssm_input,
    ssm_gate,
    input_map,
    output_map,
    step_raw,
    log_rate,
    skip_gain,
    head_gain,
    moe_gain,
    expert_ids,
    gate_weight,
    expert_up,
    expert_down,
):
    heads_loc = log_rate.shape[0]
    local_rows = residual.shape[1]
    width_loc = residual.shape[2]
    head_size = width_loc // heads_loc
    values = ssm_input[0].astype(jnp.float32).reshape(local_rows, heads_loc, head_size)
    step_size = jax.nn.softplus(step_raw[0])
    cumulative = jnp.cumsum(step_size * (-jnp.exp(log_rate))[None, :], axis=0)
    scores = jnp.einsum(
        "tn,sn->ts", output_map[0], input_map[0], preferred_element_type=jnp.float32
    )
    positions = jnp.arange(local_rows)
    causal = positions[:, None] >= positions[None, :]
    spread = cumulative[:, None, :] - cumulative[None, :, :]
    kernel = (
        jnp.where(causal[:, :, None], jnp.exp(jnp.minimum(spread, 0.0)), 0.0)
        * scores[:, :, None]
        * step_size[None, :, :]
    )
    within = jnp.einsum("tsh,shp->thp", kernel, values, precision=lax.Precision.HIGHEST)
    ending = cumulative[-1]
    carried = jnp.exp(ending[None, :] - cumulative) * step_size
    in_map_wide = input_map[0].astype(jnp.float32)
    out_map_wide = output_map[0].astype(jnp.float32)
    local_state = jnp.einsum(
        "sh,shp,sn->hpn", carried, values, in_map_wide, precision=lax.Precision.HIGHEST
    )
    total_decay = jnp.exp(ending)
    incoming = jnp.zeros_like(local_state)
    for repeat in range(lax.axis_size("ctx") - 1):
        outgoing = total_decay[:, None, None] * incoming + local_state
        incoming = shifted(outgoing.astype(jnp.bfloat16), "ctx", 1).astype(outgoing.dtype)
    across_heads = (
        jnp.einsum("tn,hpn->thp", out_map_wide, incoming, precision=lax.Precision.HIGHEST)
        * jnp.exp(cumulative)[:, :, None]
    )
    mixed_y = within + across_heads + skip_gain[None, :, None] * values
    gated = mixed_y * jax.nn.silu(
        ssm_gate[0].astype(jnp.float32).reshape(local_rows, heads_loc, head_size)
    )
    normed = (
        gated
        * lax.rsqrt(jnp.mean(gated * gated, axis=2, keepdims=True) + EPSILON)
        * head_gain.reshape(heads_loc, head_size)
    )
    hidden = (residual[0].astype(jnp.float32) + normed.reshape(local_rows, width_loc)).astype(
        jnp.bfloat16
    )
    exp_count = lax.axis_size("exp")
    my_expert = lax.axis_index("exp")
    tok_rows = local_rows // exp_count
    capacity = min(tok_rows, max(4, 4 * tok_rows // exp_count))
    model_width = width_loc * exp_count
    routes_all = expert_ids[0].reshape(exp_count, tok_rows, 2)
    slots_all = route_slots(routes_all, exp_count)
    targets_all = routes_all * capacity + slots_all
    slot_ids = jnp.arange(exp_count * capacity, dtype=jnp.int32)
    own_targets = lax.dynamic_slice_in_dim(targets_all, my_expert, 1, 0)[0]
    own_weights = lax.dynamic_slice_in_dim(
        gate_weight[0].reshape(exp_count, tok_rows, 2), my_expert, 1, 0
    )[0]
    hidden_wide = hidden.astype(jnp.float32)
    squared_values = lax.psum(jnp.sum(hidden_wide * hidden_wide, axis=1), "exp")
    gain_part = lax.dynamic_slice_in_dim(moe_gain, my_expert * width_loc, width_loc, 0)
    normal_part = (
        hidden_wide
        * lax.rsqrt(squared_values[:, None] / model_width + EPSILON)
        * gain_part[None, :]
    ).astype(jnp.bfloat16)
    placing_all = jnp.any(
        slot_ids[None, :, None, None] == targets_all[:, None, :, :], axis=3
    ).astype(jnp.bfloat16)
    outbound = jnp.einsum(
        "bqt,btc->bqc",
        placing_all,
        normal_part.reshape(exp_count, tok_rows, width_loc),
        preferred_element_type=jnp.float32,
    )
    outbound = outbound.astype(jnp.bfloat16).reshape(exp_count, exp_count, capacity, width_loc)
    arrived = lax.all_to_all(outbound, "exp", split_axis=1, concat_axis=3, tiled=True).reshape(
        exp_count * capacity, model_width
    )
    up_local = expert_up[0]
    down_local = expert_down[0]
    activated = jax.nn.silu(
        jnp.dot(
            lax.all_gather(arrived, ("dp", "ctx"), axis=0, tiled=True),
            up_local,
            preferred_element_type=jnp.float32,
        )
    ).astype(jnp.bfloat16)
    summed = lax.psum_scatter(
        jnp.dot(activated, down_local, preferred_element_type=jnp.float32).astype(jnp.bfloat16),
        ("dp", "ctx"),
        scatter_dimension=0,
        tiled=True,
    )
    sent_back = summed.reshape(exp_count, capacity, model_width)
    returned = lax.all_to_all(sent_back, "exp", split_axis=0, concat_axis=0, tiled=True).reshape(
        exp_count * capacity, model_width
    )
    picking = (own_targets.reshape(-1)[:, None] == slot_ids[None, :]).astype(jnp.bfloat16)
    chosen = jnp.dot(picking, returned, preferred_element_type=jnp.float32).reshape(
        tok_rows, 2, model_width
    )
    combined = jnp.sum(own_weights[:, :, None] * chosen, axis=1).astype(jnp.bfloat16)
    return (hidden[None], combined[None])


def softplus(raw):
    return jnp.maximum(raw, 0.0) + jnp.log1p(jnp.exp(-jnp.abs(raw)))


def iotas(rows, columns):
    shape = (rows, columns)
    return lax.broadcasted_iota(jnp.int32, shape, 0), lax.broadcasted_iota(jnp.int32, shape, 1)


def as_column(row):
    size = row.shape[1]
    down, across = iotas(size, size)
    return jnp.sum(jnp.where(down == across, row, 0.0), axis=1, keepdims=True)


def fetch(pairs, sems):
    copies = [pltpu.make_async_copy(a, b, sems.at[i]) for i, (a, b) in enumerate(pairs)]
    for copy in copies:
        copy.start()
    return copies


def pack_kernel(b_hbm, step_hbm, out_ref, b_ref, step_ref, sems):
    copies = fetch([(b_hbm, b_ref), (step_hbm, step_ref)], sems)
    rows, (heads, places) = b_ref.shape[0], step_ref.shape
    out_ref[rows:] = jnp.zeros((heads, out_ref.shape[1]), F32)
    for copy in copies:
        copy.wait()
    out_ref[:rows] = b_ref[...].astype(F32)
    out_ref[rows:, :places] = step_ref[...]


def own_kernel(
    x_hbm, gate_hbm, res_hbm, b_hbm, c_hbm, step_hbm, rate_hbm, gain_hbm, skip_hbm,
    mixed_ref, gate_ref, decay_ref, res_ref, c_ref, rate_ref, gain_ref,
    x_ref, raw_gate_ref, b_ref, step_ref, skip_ref, sems,
):
    copies = fetch(
        [
            (step_hbm, step_ref), (rate_hbm, rate_ref), (b_hbm, b_ref), (c_hbm, c_ref), (x_hbm, x_ref),
            (skip_hbm, skip_ref), (gate_hbm, raw_gate_ref), (res_hbm, res_ref), (gain_hbm, gain_ref),
        ],
        sems,
    )
    rows, width = x_ref.shape
    heads = step_ref.shape[0]
    size = width // heads
    pad = 64 - rows
    copies[0].wait()
    copies[1].wait()
    steps = softplus(step_ref[...])
    decay = steps * -jnp.exp(as_column(rate_ref[...]))
    down, across = iotas(rows, 128)
    place = across & 63
    to_row = jnp.where((down <= place) & (place < rows), -1.0, 0.0)
    to_step = jnp.where(down == place, 1.0, 0.0)
    row_part = jnp.dot(decay, to_row, precision=EXACT, preferred_element_type=F32)
    steps_twice = jnp.dot(steps, to_step, precision=EXACT, preferred_element_type=F32)
    t_row, u_col = iotas(rows, rows)
    to_col = jnp.where(u_col <= t_row, 1.0, 0.0)
    col_part = lax.dot_general(to_col, decay, LAST, precision=EXACT, preferred_element_type=F32)
    copies[2].wait()
    copies[3].wait()
    zeros = jnp.zeros((pad, b_ref.shape[1]), BF16)
    maps = jnp.concatenate([b_ref[...], zeros, b_ref[...], zeros], axis=0)
    scores = lax.dot_general(c_ref[...], maps, LAST, preferred_element_type=F32)
    scores = jnp.where(place <= down, scores, 0.0)
    lane = lax.broadcasted_iota(jnp.int32, (1, 128), 1)
    low = lane < size
    zeros = jnp.zeros((pad, 128), BF16)
    for copy in copies[4:]:
        copy.wait()
    skips = as_column(skip_ref[...])
    for pair in range(width // 128):
        cut = slice(pair * 128, (pair + 1) * 128)
        first, second = 2 * pair, 2 * pair + 1
        x_own = x_ref[:, cut]
        column = jnp.where(low, col_part[:, first : first + 1], col_part[:, second : second + 1])
        row = jnp.where(low, row_part[first : first + 1], row_part[second : second + 1])
        step = jnp.where(low, steps_twice[first : first + 1], steps_twice[second : second + 1])
        kernel = jnp.exp(jnp.minimum(column + row, 0.0)) * scores * step
        high = kernel.astype(BF16)
        rest = (kernel - high.astype(F32)).astype(BF16)
        none = jnp.zeros_like(x_own)
        values = jnp.concatenate(
            [jnp.where(low, x_own, none), zeros, jnp.where(low, none, x_own), zeros], axis=0
        )
        mixed = jnp.dot(jnp.concatenate([high, rest], axis=0), values, preferred_element_type=F32)
        skip = jnp.where(low, skips[first : first + 1], skips[second : second + 1])
        mixed_ref[:, cut] = mixed[:rows] + mixed[rows:] + skip * x_own.astype(F32)
        gate = raw_gate_ref[:, cut].astype(F32)
        gate_ref[:, cut] = gate / (1.0 + jnp.exp(-gate))
        decay_ref[:, cut] = jnp.exp(column)


def mixer_kernel(
    mixed_ref, gate_ref, decay_ref, res_ref, c_ref, rate_ref, gain_ref, x_ref, pack_ref, out_ref
):
    rows, width = x_ref.shape
    heads = rate_ref.shape[1]
    size = width // heads
    steps = softplus(pack_ref[rows:, :rows])
    decay = steps * -jnp.exp(as_column(rate_ref[...]))
    down, across = iotas(rows, rows)
    after = jnp.where(down > across, 1.0, 0.0)
    same = jnp.where(down == across, 1.0, 0.0)
    carried = jnp.exp(jnp.dot(decay, after, precision=EXACT, preferred_element_type=F32)) * steps
    carried = lax.dot_general(same, carried, LAST, precision=EXACT, preferred_element_type=F32)
    scores = lax.dot_general(
        c_ref[...], pack_ref[:rows].astype(BF16), LAST, preferred_element_type=F32
    )
    s_high = scores.astype(BF16)
    s_rest = (scores - s_high.astype(F32)).astype(BF16)
    s_both = jnp.concatenate([s_high, s_rest], axis=0)
    low = lax.broadcasted_iota(jnp.int32, (1, 128), 1) < size
    for pair in range(width // 128):
        cut = slice(pair * 128, (pair + 1) * 128)
        first, second = 2 * pair, 2 * pair + 1
        weight = jnp.where(low, carried[:, first : first + 1], carried[:, second : second + 1])
        values = weight * x_ref[:, cut].astype(F32)
        v_high = values.astype(BF16)
        v_rest = (values - v_high.astype(F32)).astype(BF16)
        cross = jnp.dot(s_both, v_high, preferred_element_type=F32)
        cross = cross[:rows] + cross[rows:] + jnp.dot(s_high, v_rest, preferred_element_type=F32)
        gated = (mixed_ref[:, cut] + decay_ref[:, cut] * cross) * gate_ref[:, cut]
        square = gated * gated
        mean_low = jnp.sum(jnp.where(low, square, 0.0), axis=1, keepdims=True) / size
        mean_high = jnp.sum(jnp.where(low, 0.0, square), axis=1, keepdims=True) / size
        scale = lax.rsqrt(jnp.where(low, mean_low, mean_high) + EPSILON)
        normed = gated * scale * gain_ref[:, cut]
        out_ref[:, cut] = (res_ref[:, cut].astype(F32) + normed).astype(BF16)


def add_up(blocks, gain, weights, scaled):
    rows, width = blocks[0].shape
    squares = []
    for i, block in enumerate(blocks):
        wide = block[...].astype(F32)
        squares.append(jnp.sum(wide * wide, axis=1, keepdims=True))
        scaled[i * rows : (i + 1) * rows] = (wide * gain).astype(BF16)
    return jnp.dot(scaled[...], weights, preferred_element_type=F32), jnp.concatenate(squares, axis=0)


def slice_of(expert, k, up_ref, gain_ref, width):
    cut = pl.ds(pl.multiple_of((lax.axis_index(expert) ^ k) * width, width), width)
    return gain_ref[:, cut], up_ref[cut]


def first_up_kernel(expert, count, *refs):
    blocks, (up_ref, gain_ref, ids_hbm, weight_hbm) = refs[:count], refs[count : count + 4]
    total_ref, square_ref, route_ref, hidden_hbm = refs[count + 4 : count + 8]
    ids, weights, scaled, sems = refs[count + 8 :]
    copies = fetch([(ids_hbm, ids), (weight_hbm, weights), (blocks[0], hidden_hbm)], sems)
    width = blocks[0].shape[1]
    gain, up = slice_of(expert, 0, up_ref, gain_ref, width)
    total_ref[...], square_ref[...] = add_up(blocks, gain, up, scaled)
    for copy in copies:
        copy.wait()
    row = jnp.sum(
        jnp.where(ids[...] == lax.axis_index(expert), weights[...], 0.0), axis=0, keepdims=True
    )
    route_ref[...] = as_column(row)


def second_up_kernel(expert, count, rows, model, *refs):
    blocks = refs[:count]
    total_ref, square_ref, up_ref, gain_ref, out_ref, scaled = refs[count:]
    width = scaled.shape[1]
    total, squares = total_ref[rows], square_ref[rows]
    for k in range(1, model // width):
        cut = slice((k - 1) * width, k * width)
        gain, up = slice_of(expert, k, up_ref, gain_ref, width)
        part, square = add_up([b.at[:, cut] for b in blocks], gain, up, scaled)
        total += part
        squares += square
    value = total * lax.rsqrt(squares / model + EPSILON)
    out_ref[...] = (value / (1.0 + jnp.exp(-value))).astype(BF16)


def down_kernel(columns, act_ref, down_ref, out_ref):
    out_ref[...] = jnp.dot(
        act_ref[...], down_ref[:, columns], preferred_element_type=F32
    ).astype(BF16)


def join_kernel(*refs):
    blocks, out_ref = refs[:-1], refs[-1]
    width = blocks[0].shape[1]
    for i, block in enumerate(blocks):
        out_ref[:, i * width : (i + 1) * width] = block[...]


def add_kernel(own_ref, other_ref, *outs):
    rows = outs[0].shape[0]
    for i, out in enumerate(outs):
        cut = slice(i * rows, (i + 1) * rows)
        out[...] = (own_ref[cut].astype(F32) + other_ref[cut].astype(F32)).astype(BF16)


def weigh_kernel(expert, own_ref, *refs):
    others, route_ref, outs = refs[:3], refs[3], refs[4:]
    me = lax.axis_index(expert)
    rows, columns = own_ref.shape
    parts = len(outs)
    keep, width = rows // parts, columns // parts
    total = own_ref[...].astype(F32)
    for other in others:
        total += other[...].astype(F32)
    total = (total * route_ref[...]).astype(BF16)
    place, source = iotas(parts * rows, parts * rows)
    part, place = place // rows, place % rows
    wanted = place // keep * rows + (part ^ me) * keep + place % keep
    stacked = jnp.concatenate([total[:, j * width : (j + 1) * width] for j in range(parts)], axis=0)
    pick = jnp.where(source == wanted, 1.0, 0.0).astype(BF16)
    picked = jnp.dot(pick, stacked, preferred_element_type=F32)
    for k, out in enumerate(outs):
        out[...] = picked[k * rows : (k + 1) * rows].astype(BF16)


def last_kernel(count, *refs):
    terms, out_ref = refs[:-1], refs[-1]
    keep, start = out_ref.shape[0], 0
    for i in range(0, len(terms), count):
        total = sum(term[...].astype(F32) for term in terms[i : i + count])
        width = total.shape[1]
        for j in range(count):
            out_ref[:, start : start + width] = total[j * keep : (j + 1) * keep].astype(BF16)
            start += width


def call(kernel, outs, inputs, name, scratch=(), in_hbm=(), out_hbm=(), limit=16, us=0.01, after=()):
    vmem, hbm = pl.BlockSpec(memory_space=pltpu.VMEM), pl.BlockSpec(memory_space=pltpu.HBM)
    inputs = [
        pltpu.with_memory_space_constraint(a, pltpu.HBM) if i in in_hbm else a for i, a in enumerate(inputs)
    ]
    given, extra = len(inputs), len(after)

    def without(*refs):
        return kernel(*refs[:given], *refs[given + extra :])

    return pl.pallas_call(
        without,
        out_shape=[jax.ShapeDtypeStruct(shape, dtype) for shape, dtype in outs],
        in_specs=[hbm if i in in_hbm else vmem for i in range(given)]
        + [pl.BlockSpec(memory_space=pl.ANY)] * extra,
        out_specs=[hbm if i in out_hbm else vmem for i in range(len(outs))],
        scratch_shapes=scratch,
        compiler_params=pltpu.CompilerParams(vmem_limit_bytes=limit * MIB),
        cost_estimate=pl.CostEstimate(
            flops=int(us * 1e9), bytes_accessed=int(us * 3e6), transcendentals=0
        ),
        name=name,
    )(*inputs, *after)


def plane_body(
    residual, ssm_input, ssm_gate, input_map, output_map, step_raw, log_rate, skip_gain, head_gain,
    moe_gain, expert_ids, gate_weight, expert_up, expert_down,
):
    rows, width = residual.shape[1:]
    heads = log_rate.shape[0]
    state = input_map.shape[2]
    experts = lax.axis_size("exp")
    model = experts * width
    units = expert_up.shape[2]
    plane = ("dp", "ctx")

    def along_z(block, k):
        return lax.ppermute(block, "exp", [(i, i ^ k) for i in range(experts)])

    def in_plane(block, x, y, core):
        route = [
            (d * 2 + c, (d ^ (y * 2) ^ core) * 2 + (c ^ x)) for d in range(4) for c in range(2)
        ]
        return lax.ppermute(block, plane, route)

    step_t = step_raw[0].T
    (packed,) = call(
        pack_kernel,
        [((rows + heads, state), F32)],
        [input_map[0], step_t],
        "pack",
        scratch=[
            pltpu.VMEM((rows, state), BF16), pltpu.VMEM((heads, rows), F32), pltpu.SemaphoreType.DMA((2,)),
        ],
        in_hbm=range(2),
    )
    before = [lax.ppermute(a, "ctx", [(0, 1)]) for a in (ssm_input[0], packed)]
    wide, flat = (rows, width), (rows, state)
    own = call(
        own_kernel,
        [(wide, F32), (wide, F32), (wide, F32), (wide, BF16), (flat, BF16), ((1, heads), F32), ((1, width), F32)],
        [
            ssm_input[0], ssm_gate[0], residual[0], input_map[0], output_map[0], step_t,
            log_rate[None], head_gain[None], skip_gain[None],
        ],
        "mixer_own",
        scratch=[
            pltpu.VMEM(wide, BF16), pltpu.VMEM(wide, BF16), pltpu.VMEM(flat, BF16),
            pltpu.VMEM((heads, rows), F32), pltpu.VMEM((1, heads), F32), pltpu.SemaphoreType.DMA((9,)),
        ],
        in_hbm=range(9),
    )
    (sent,) = call(mixer_kernel, [(wide, BF16)], [*own, *before], "mixer")
    chips = ((0, 0), (1, 0), (0, 1), (1, 1))

    def joined(blocks, name, after=(), us=0.01):
        shape = (rows, width * len(blocks))
        return call(join_kernel, [(shape, BF16)], blocks, name, after=after, us=us)[0]

    arrived_z = [along_z(sent, k) for k in range(1, experts)]
    near = [sent] + [in_plane(sent, x, y, 0) for x, y in chips[1:]]
    corner = [along_z(near[3], k) for k in CORNER]
    rest = joined(arrived_z, "join_z", us=JOIN)
    second = [in_plane(rest, x, y, 0) for x, y in chips[1:3]]
    if len(CORNER) < 3:
        corner.append(in_plane(arrived_z[2], 1, 1, 0))
    first = near + [in_plane(block, 0, 0, 1) for block in near]
    half = len(near) * rows
    count = 2 * half
    up, gain, down = expert_up[0], moe_gain[None], expert_down[0]
    total, squares, route, hidden = call(
        functools.partial(first_up_kernel, "exp", len(first)),
        [((count, units), F32), ((count, 1), F32), ((rows, 1), F32), (wide, BF16)],
        [*first, up, gain, expert_ids[0].T, gate_weight[0].T],
        "up_first",
        scratch=[
            pltpu.VMEM((2, rows), jnp.int32), pltpu.VMEM((2, rows), F32),
            pltpu.VMEM((count, width), BF16), pltpu.SemaphoreType.DMA((3,)),
        ],
        in_hbm=range(len(first) + 2, len(first) + 4),
        out_hbm=(3,),
        limit=32,
    )
    *others, total = lax.optimization_barrier((*second, *corner, total))
    second = [rest, *others[:2], joined(others[2:], "join_corner", us=10.0)]
    activated = []
    for i, blocks in enumerate((second, [in_plane(block, 0, 0, 1) for block in second])):
        activated += call(
            functools.partial(second_up_kernel, "exp", len(blocks), slice(i * half, (i + 1) * half), model),
            [((half, units), BF16)],
            [*blocks, total, squares, up, gain],
            "up_second",
            scratch=[pltpu.VMEM((half, width), BF16)],
            limit=24,
            after=activated,
        )
    keep = rows // experts
    middle = model * 5 // 8
    cuts = (slice(0, middle), slice(middle, model))

    def down_part(i, columns, after, us=0.01):
        return call(
            functools.partial(down_kernel, columns),
            [((half, columns.stop - columns.start), BF16)],
            [activated[i], down],
            "down",
            after=after,
            us=us,
        )

    terms, done = [], []
    for columns in cuts:
        cut = columns.stop - columns.start
        (sibling,) = down_part(1, columns, done)
        (mine,) = down_part(0, columns, [sibling])
        summed = call(
            add_kernel, [((rows, cut), BF16)] * 4, [mine, in_plane(sibling, 0, 0, 1)], "add_cores"
        )
        done = summed[:1]
        returned = [in_plane(summed[i], x, y, 0) for i, (x, y) in enumerate(chips) if i]
        slices = call(
            functools.partial(weigh_kernel, "exp"),
            [((rows, cut // experts), BF16)] * experts,
            [summed[0], *returned, route],
            "weigh",
            after=terms[:1],
        )
        terms += [slices[0]] + [along_z(slices[k], k) for k in range(experts - 1, 0, -1)]
    (out,) = call(
        functools.partial(last_kernel, experts), [((rows // experts, model), BF16)], terms, "last"
    )
    return (hidden[None], out[None])


def solution(mesh):
    placed = (
        P("dp", "ctx", "exp"),
        P("dp", "ctx", "exp"),
        P("dp", "ctx", "exp"),
        P("dp", "ctx", None),
        P("dp", "ctx", None),
        P("dp", "ctx", "exp"),
        P("exp"),
        P("exp"),
        P("exp"),
        P(),
        P("dp", "ctx", None),
        P("dp", "ctx", None),
        P("exp", None, ("dp", "ctx")),
        P("exp", ("dp", "ctx"), None),
    )
    sizes = tuple(mesh.shape[axis] for axis in ("dp", "ctx", "exp"))
    return jax.shard_map(
        plane_body if sizes == (4, 2, 4) else body,
        mesh=mesh,
        in_specs=placed,
        out_specs=(P("dp", "ctx", "exp"), P("dp", ("ctx", "exp"), None)),
        check_vma=False,
    )
```

```python
import functools

import jax
import jax.numpy as jnp
from jax import lax
from jax.experimental import pallas as pl
from jax.experimental.pallas import tpu as pltpu
from jax.sharding import PartitionSpec as P

EPSILON = 1e-05
BF16 = jnp.bfloat16
CORNER = (1, 2)
JOIN = 10.0
F32 = jnp.float32
MIB = 1 << 20
EXACT = lax.Precision.HIGHEST
LAST = (((1,), (1,)), ((), ()))


def shifted(block, axis, distance):
    devices = range(lax.axis_size(axis))
    route = [(i - distance, i) for i in devices if i - distance in devices]
    return lax.ppermute(block, axis, route)


def route_slots(routes, experts):
    blocks = routes.shape[0]
    ordered = routes.reshape(blocks, -1)
    matches = (ordered[:, :, None] == jnp.arange(experts, dtype=jnp.int32)[None, None, :]).astype(
        jnp.int32
    )
    earlier = jnp.cumsum(matches, axis=1) - matches
    return jnp.sum(earlier * matches, axis=2).reshape(routes.shape)


def body(
    residual,
    ssm_input,
    ssm_gate,
    input_map,
    output_map,
    step_raw,
    log_rate,
    skip_gain,
    head_gain,
    moe_gain,
    expert_ids,
    gate_weight,
    expert_up,
    expert_down,
):
    heads_loc = log_rate.shape[0]
    local_rows = residual.shape[1]
    width_loc = residual.shape[2]
    head_size = width_loc // heads_loc
    values = ssm_input[0].astype(jnp.float32).reshape(local_rows, heads_loc, head_size)
    step_size = jax.nn.softplus(step_raw[0])
    cumulative = jnp.cumsum(step_size * (-jnp.exp(log_rate))[None, :], axis=0)
    scores = jnp.einsum(
        "tn,sn->ts", output_map[0], input_map[0], preferred_element_type=jnp.float32
    )
    positions = jnp.arange(local_rows)
    causal = positions[:, None] >= positions[None, :]
    spread = cumulative[:, None, :] - cumulative[None, :, :]
    kernel = (
        jnp.where(causal[:, :, None], jnp.exp(jnp.minimum(spread, 0.0)), 0.0)
        * scores[:, :, None]
        * step_size[None, :, :]
    )
    within = jnp.einsum("tsh,shp->thp", kernel, values, precision=lax.Precision.HIGHEST)
    ending = cumulative[-1]
    carried = jnp.exp(ending[None, :] - cumulative) * step_size
    in_map_wide = input_map[0].astype(jnp.float32)
    out_map_wide = output_map[0].astype(jnp.float32)
    local_state = jnp.einsum(
        "sh,shp,sn->hpn", carried, values, in_map_wide, precision=lax.Precision.HIGHEST
    )
    total_decay = jnp.exp(ending)
    incoming = jnp.zeros_like(local_state)
    for repeat in range(lax.axis_size("ctx") - 1):
        outgoing = total_decay[:, None, None] * incoming + local_state
        incoming = shifted(outgoing.astype(jnp.bfloat16), "ctx", 1).astype(outgoing.dtype)
    across_heads = (
        jnp.einsum("tn,hpn->thp", out_map_wide, incoming, precision=lax.Precision.HIGHEST)
        * jnp.exp(cumulative)[:, :, None]
    )
    mixed_y = within + across_heads + skip_gain[None, :, None] * values
    gated = mixed_y * jax.nn.silu(
        ssm_gate[0].astype(jnp.float32).reshape(local_rows, heads_loc, head_size)
    )
    normed = (
        gated
        * lax.rsqrt(jnp.mean(gated * gated, axis=2, keepdims=True) + EPSILON)
        * head_gain.reshape(heads_loc, head_size)
    )
    hidden = (residual[0].astype(jnp.float32) + normed.reshape(local_rows, width_loc)).astype(
        jnp.bfloat16
    )
    exp_count = lax.axis_size("exp")
    my_expert = lax.axis_index("exp")
    tok_rows = local_rows // exp_count
    capacity = min(tok_rows, max(4, 4 * tok_rows // exp_count))
    model_width = width_loc * exp_count
    routes_all = expert_ids[0].reshape(exp_count, tok_rows, 2)
    slots_all = route_slots(routes_all, exp_count)
    targets_all = routes_all * capacity + slots_all
    slot_ids = jnp.arange(exp_count * capacity, dtype=jnp.int32)
    own_targets = lax.dynamic_slice_in_dim(targets_all, my_expert, 1, 0)[0]
    own_weights = lax.dynamic_slice_in_dim(
        gate_weight[0].reshape(exp_count, tok_rows, 2), my_expert, 1, 0
    )[0]
    hidden_wide = hidden.astype(jnp.float32)
    squared_values = lax.psum(jnp.sum(hidden_wide * hidden_wide, axis=1), "exp")
    gain_part = lax.dynamic_slice_in_dim(moe_gain, my_expert * width_loc, width_loc, 0)
    normal_part = (
        hidden_wide
        * lax.rsqrt(squared_values[:, None] / model_width + EPSILON)
        * gain_part[None, :]
    ).astype(jnp.bfloat16)
    placing_all = jnp.any(
        slot_ids[None, :, None, None] == targets_all[:, None, :, :], axis=3
    ).astype(jnp.bfloat16)
    outbound = jnp.einsum(
        "bqt,btc->bqc",
        placing_all,
        normal_part.reshape(exp_count, tok_rows, width_loc),
        preferred_element_type=jnp.float32,
    )
    outbound = outbound.astype(jnp.bfloat16).reshape(exp_count, exp_count, capacity, width_loc)
    arrived = lax.all_to_all(outbound, "exp", split_axis=1, concat_axis=3, tiled=True).reshape(
        exp_count * capacity, model_width
    )
    up_local = expert_up[0]
    down_local = expert_down[0]
    activated = jax.nn.silu(
        jnp.dot(
            lax.all_gather(arrived, ("dp", "ctx"), axis=0, tiled=True),
            up_local,
            preferred_element_type=jnp.float32,
        )
    ).astype(jnp.bfloat16)
    summed = lax.psum_scatter(
        jnp.dot(activated, down_local, preferred_element_type=jnp.float32).astype(jnp.bfloat16),
        ("dp", "ctx"),
        scatter_dimension=0,
        tiled=True,
    )
    sent_back = summed.reshape(exp_count, capacity, model_width)
    returned = lax.all_to_all(sent_back, "exp", split_axis=0, concat_axis=0, tiled=True).reshape(
        exp_count * capacity, model_width
    )
    picking = (own_targets.reshape(-1)[:, None] == slot_ids[None, :]).astype(jnp.bfloat16)
    chosen = jnp.dot(picking, returned, preferred_element_type=jnp.float32).reshape(
        tok_rows, 2, model_width
    )
    combined = jnp.sum(own_weights[:, :, None] * chosen, axis=1).astype(jnp.bfloat16)
    return (hidden[None], combined[None])


def softplus(raw):
    return jnp.maximum(raw, 0.0) + jnp.log1p(jnp.exp(-jnp.abs(raw)))


def iotas(rows, columns):
    shape = (rows, columns)
    return lax.broadcasted_iota(jnp.int32, shape, 0), lax.broadcasted_iota(jnp.int32, shape, 1)


def as_column(row):
    size = row.shape[1]
    down, across = iotas(size, size)
    return jnp.sum(jnp.where(down == across, row, 0.0), axis=1, keepdims=True)


def fetch(pairs, sems):
    copies = [pltpu.make_async_copy(a, b, sems.at[i]) for i, (a, b) in enumerate(pairs)]
    for copy in copies:
        copy.start()
    return copies


def pack_kernel(b_hbm, step_hbm, out_ref, b_ref, step_ref, sems):
    copies = fetch([(b_hbm, b_ref), (step_hbm, step_ref)], sems)
    rows, (heads, places) = b_ref.shape[0], step_ref.shape
    out_ref[rows:] = jnp.zeros((heads, out_ref.shape[1]), F32)
    for copy in copies:
        copy.wait()
    out_ref[:rows] = b_ref[...].astype(F32)
    out_ref[rows:, :places] = step_ref[...]


def own_kernel(
    x_hbm, gate_hbm, res_hbm, b_hbm, c_hbm, step_hbm, rate_hbm, gain_hbm, skip_hbm,
    mixed_ref, gate_ref, decay_ref, res_ref, c_ref, rate_ref, gain_ref,
    x_ref, raw_gate_ref, b_ref, step_ref, skip_ref, sems,
):
    copies = fetch(
        [
            (step_hbm, step_ref), (rate_hbm, rate_ref), (b_hbm, b_ref), (c_hbm, c_ref), (x_hbm, x_ref),
            (skip_hbm, skip_ref), (gate_hbm, raw_gate_ref), (res_hbm, res_ref), (gain_hbm, gain_ref),
        ],
        sems,
    )
    rows, width = x_ref.shape
    heads = step_ref.shape[0]
    size = width // heads
    pad = 64 - rows
    copies[0].wait()
    copies[1].wait()
    steps = softplus(step_ref[...])
    decay = steps * -jnp.exp(as_column(rate_ref[...]))
    down, across = iotas(rows, 128)
    place = across & 63
    to_row = jnp.where((down <= place) & (place < rows), -1.0, 0.0)
    to_step = jnp.where(down == place, 1.0, 0.0)
    row_part = jnp.dot(decay, to_row, precision=EXACT, preferred_element_type=F32)
    steps_twice = jnp.dot(steps, to_step, precision=EXACT, preferred_element_type=F32)
    t_row, u_col = iotas(rows, rows)
    to_col = jnp.where(u_col <= t_row, 1.0, 0.0)
    col_part = lax.dot_general(to_col, decay, LAST, precision=EXACT, preferred_element_type=F32)
    copies[2].wait()
    copies[3].wait()
    zeros = jnp.zeros((pad, b_ref.shape[1]), BF16)
    maps = jnp.concatenate([b_ref[...], zeros, b_ref[...], zeros], axis=0)
    scores = lax.dot_general(c_ref[...], maps, LAST, preferred_element_type=F32)
    scores = jnp.where(place <= down, scores, 0.0)
    lane = lax.broadcasted_iota(jnp.int32, (1, 128), 1)
    low = lane < size
    zeros = jnp.zeros((pad, 128), BF16)
    for copy in copies[4:]:
        copy.wait()
    skips = as_column(skip_ref[...])
    for pair in range(width // 128):
        cut = slice(pair * 128, (pair + 1) * 128)
        first, second = 2 * pair, 2 * pair + 1
        x_own = x_ref[:, cut]
        column = jnp.where(low, col_part[:, first : first + 1], col_part[:, second : second + 1])
        row = jnp.where(low, row_part[first : first + 1], row_part[second : second + 1])
        step = jnp.where(low, steps_twice[first : first + 1], steps_twice[second : second + 1])
        kernel = jnp.exp(jnp.minimum(column + row, 0.0)) * scores * step
        high = kernel.astype(BF16)
        rest = (kernel - high.astype(F32)).astype(BF16)
        none = jnp.zeros_like(x_own)
        values = jnp.concatenate(
            [jnp.where(low, x_own, none), zeros, jnp.where(low, none, x_own), zeros], axis=0
        )
        mixed = jnp.dot(jnp.concatenate([high, rest], axis=0), values, preferred_element_type=F32)
        skip = jnp.where(low, skips[first : first + 1], skips[second : second + 1])
        mixed_ref[:, cut] = mixed[:rows] + mixed[rows:] + skip * x_own.astype(F32)
        gate = raw_gate_ref[:, cut].astype(F32)
        gate_ref[:, cut] = gate / (1.0 + jnp.exp(-gate))
        decay_ref[:, cut] = jnp.exp(column)


def mixer_kernel(
    mixed_ref, gate_ref, decay_ref, res_ref, c_ref, rate_ref, gain_ref, x_ref, pack_ref, out_ref
):
    rows, width = x_ref.shape
    heads = rate_ref.shape[1]
    size = width // heads
    steps = softplus(pack_ref[rows:, :rows])
    decay = steps * -jnp.exp(as_column(rate_ref[...]))
    down, across = iotas(rows, rows)
    after = jnp.where(down > across, 1.0, 0.0)
    same = jnp.where(down == across, 1.0, 0.0)
    carried = jnp.exp(jnp.dot(decay, after, precision=EXACT, preferred_element_type=F32)) * steps
    carried = lax.dot_general(same, carried, LAST, precision=EXACT, preferred_element_type=F32)
    scores = lax.dot_general(
        c_ref[...], pack_ref[:rows].astype(BF16), LAST, preferred_element_type=F32
    )
    s_high = scores.astype(BF16)
    s_rest = (scores - s_high.astype(F32)).astype(BF16)
    s_both = jnp.concatenate([s_high, s_rest], axis=0)
    low = lax.broadcasted_iota(jnp.int32, (1, 128), 1) < size
    for pair in range(width // 128):
        cut = slice(pair * 128, (pair + 1) * 128)
        first, second = 2 * pair, 2 * pair + 1
        weight = jnp.where(low, carried[:, first : first + 1], carried[:, second : second + 1])
        values = weight * x_ref[:, cut].astype(F32)
        v_high = values.astype(BF16)
        v_rest = (values - v_high.astype(F32)).astype(BF16)
        cross = jnp.dot(s_both, v_high, preferred_element_type=F32)
        cross = cross[:rows] + cross[rows:] + jnp.dot(s_high, v_rest, preferred_element_type=F32)
        gated = (mixed_ref[:, cut] + decay_ref[:, cut] * cross) * gate_ref[:, cut]
        square = gated * gated
        mean_low = jnp.sum(jnp.where(low, square, 0.0), axis=1, keepdims=True) / size
        mean_high = jnp.sum(jnp.where(low, 0.0, square), axis=1, keepdims=True) / size
        scale = lax.rsqrt(jnp.where(low, mean_low, mean_high) + EPSILON)
        normed = gated * scale * gain_ref[:, cut]
        out_ref[:, cut] = (res_ref[:, cut].astype(F32) + normed).astype(BF16)


def add_up(blocks, gain, weights, scaled):
    rows, width = blocks[0].shape
    squares = []
    for i, block in enumerate(blocks):
        wide = block[...].astype(F32)
        squares.append(jnp.sum(wide * wide, axis=1, keepdims=True))
        scaled[i * rows : (i + 1) * rows] = (wide * gain).astype(BF16)
    return jnp.dot(scaled[...], weights, preferred_element_type=F32), jnp.concatenate(squares, axis=0)


def slice_of(expert, k, up_ref, gain_ref, width):
    cut = pl.ds(pl.multiple_of((lax.axis_index(expert) ^ k) * width, width), width)
    return gain_ref[:, cut], up_ref[cut]


def first_up_kernel(expert, count, *refs):
    blocks, (up_ref, gain_ref, ids_hbm, weight_hbm) = refs[:count], refs[count : count + 4]
    total_ref, square_ref, route_ref, hidden_hbm = refs[count + 4 : count + 8]
    ids, weights, scaled, sems = refs[count + 8 :]
    copies = fetch([(ids_hbm, ids), (weight_hbm, weights), (blocks[0], hidden_hbm)], sems)
    width = blocks[0].shape[1]
    gain, up = slice_of(expert, 0, up_ref, gain_ref, width)
    total_ref[...], square_ref[...] = add_up(blocks, gain, up, scaled)
    for copy in copies:
        copy.wait()
    row = jnp.sum(
        jnp.where(ids[...] == lax.axis_index(expert), weights[...], 0.0), axis=0, keepdims=True
    )
    route_ref[...] = as_column(row)


def second_up_kernel(expert, count, rows, model, *refs):
    blocks = refs[:count]
    total_ref, square_ref, up_ref, gain_ref, out_ref, scaled = refs[count:]
    width = scaled.shape[1]
    total, squares = total_ref[rows], square_ref[rows]
    for k in range(1, model // width):
        cut = slice((k - 1) * width, k * width)
        gain, up = slice_of(expert, k, up_ref, gain_ref, width)
        part, square = add_up([b.at[:, cut] for b in blocks], gain, up, scaled)
        total += part
        squares += square
    value = total * lax.rsqrt(squares / model + EPSILON)
    out_ref[...] = (value / (1.0 + jnp.exp(-value))).astype(BF16)


def down_kernel(columns, act_ref, down_ref, out_ref):
    out_ref[...] = jnp.dot(
        act_ref[...], down_ref[:, columns], preferred_element_type=F32
    ).astype(BF16)


def two_down_kernel(own_columns, other_columns, own_ref, other_ref, down_ref, own_out_ref, other_out_ref):
    down_kernel(other_columns, other_ref, down_ref, other_out_ref)
    down_kernel(own_columns, own_ref, down_ref, own_out_ref)


def join_kernel(*refs):
    blocks, out_ref = refs[:-1], refs[-1]
    width = blocks[0].shape[1]
    for i, block in enumerate(blocks):
        out_ref[:, i * width : (i + 1) * width] = block[...]


def add_kernel(own_ref, other_ref, *outs):
    rows = outs[0].shape[0]
    for i, out in enumerate(outs):
        cut = slice(i * rows, (i + 1) * rows)
        out[...] = (own_ref[cut].astype(F32) + other_ref[cut].astype(F32)).astype(BF16)


def weigh_kernel(expert, own_ref, *refs):
    others, route_ref, outs = refs[:3], refs[3], refs[4:]
    me = lax.axis_index(expert)
    rows, columns = own_ref.shape
    parts = len(outs)
    keep, width = rows // parts, columns // parts
    total = own_ref[...].astype(F32)
    for other in others:
        total += other[...].astype(F32)
    total = (total * route_ref[...]).astype(BF16)
    place, source = iotas(parts * rows, parts * rows)
    part, place = place // rows, place % rows
    wanted = place // keep * rows + (part ^ me) * keep + place % keep
    stacked = jnp.concatenate([total[:, j * width : (j + 1) * width] for j in range(parts)], axis=0)
    pick = jnp.where(source == wanted, 1.0, 0.0).astype(BF16)
    picked = jnp.dot(pick, stacked, preferred_element_type=F32)
    for k, out in enumerate(outs):
        out[...] = picked[k * rows : (k + 1) * rows].astype(BF16)


def last_kernel(count, *refs):
    terms, out_ref = refs[:-1], refs[-1]
    keep, start = out_ref.shape[0], 0
    for i in range(0, len(terms), count):
        total = sum(term[...].astype(F32) for term in terms[i : i + count])
        width = total.shape[1]
        for j in range(count):
            out_ref[:, start : start + width] = total[j * keep : (j + 1) * keep].astype(BF16)
            start += width


def call(kernel, outs, inputs, name, scratch=(), in_hbm=(), out_hbm=(), limit=16, us=0.01, after=()):
    vmem, hbm = pl.BlockSpec(memory_space=pltpu.VMEM), pl.BlockSpec(memory_space=pltpu.HBM)
    inputs = [
        pltpu.with_memory_space_constraint(a, pltpu.HBM) if i in in_hbm else a for i, a in enumerate(inputs)
    ]
    given, extra = len(inputs), len(after)

    def without(*refs):
        return kernel(*refs[:given], *refs[given + extra :])

    return pl.pallas_call(
        without,
        out_shape=[jax.ShapeDtypeStruct(shape, dtype) for shape, dtype in outs],
        in_specs=[hbm if i in in_hbm else vmem for i in range(given)]
        + [pl.BlockSpec(memory_space=pl.ANY)] * extra,
        out_specs=[hbm if i in out_hbm else vmem for i in range(len(outs))],
        scratch_shapes=scratch,
        compiler_params=pltpu.CompilerParams(vmem_limit_bytes=limit * MIB),
        cost_estimate=pl.CostEstimate(
            flops=int(us * 1e9), bytes_accessed=int(us * 3e6), transcendentals=0
        ),
        name=name,
    )(*inputs, *after)


def plane_body(
    residual, ssm_input, ssm_gate, input_map, output_map, step_raw, log_rate, skip_gain, head_gain,
    moe_gain, expert_ids, gate_weight, expert_up, expert_down,
):
    rows, width = residual.shape[1:]
    heads = log_rate.shape[0]
    state = input_map.shape[2]
    experts = lax.axis_size("exp")
    model = experts * width
    units = expert_up.shape[2]
    plane = ("dp", "ctx")

    def along_z(block, k):
        return lax.ppermute(block, "exp", [(i, i ^ k) for i in range(experts)])

    def in_plane(block, x, y, core):
        route = [
            (d * 2 + c, (d ^ (y * 2) ^ core) * 2 + (c ^ x)) for d in range(4) for c in range(2)
        ]
        return lax.ppermute(block, plane, route)

    step_t = step_raw[0].T
    (packed,) = call(
        pack_kernel,
        [((rows + heads, state), F32)],
        [input_map[0], step_t],
        "pack",
        scratch=[
            pltpu.VMEM((rows, state), BF16), pltpu.VMEM((heads, rows), F32), pltpu.SemaphoreType.DMA((2,)),
        ],
        in_hbm=range(2),
    )
    before = [lax.ppermute(a, "ctx", [(0, 1)]) for a in (ssm_input[0], packed)]
    wide, flat = (rows, width), (rows, state)
    own = call(
        own_kernel,
        [(wide, F32), (wide, F32), (wide, F32), (wide, BF16), (flat, BF16), ((1, heads), F32), ((1, width), F32)],
        [
            ssm_input[0], ssm_gate[0], residual[0], input_map[0], output_map[0], step_t,
            log_rate[None], head_gain[None], skip_gain[None],
        ],
        "mixer_own",
        scratch=[
            pltpu.VMEM(wide, BF16), pltpu.VMEM(wide, BF16), pltpu.VMEM(flat, BF16),
            pltpu.VMEM((heads, rows), F32), pltpu.VMEM((1, heads), F32), pltpu.SemaphoreType.DMA((9,)),
        ],
        in_hbm=range(9),
    )
    (sent,) = call(mixer_kernel, [(wide, BF16)], [*own, *before], "mixer")
    chips = ((0, 0), (1, 0), (0, 1), (1, 1))

    def joined(blocks, name, after=(), us=0.01):
        shape = (rows, width * len(blocks))
        return call(join_kernel, [(shape, BF16)], blocks, name, after=after, us=us)[0]

    arrived_z = [along_z(sent, k) for k in range(1, experts)]
    near = [sent] + [in_plane(sent, x, y, 0) for x, y in chips[1:]]
    corner = [along_z(near[3], k) for k in CORNER]
    rest = joined(arrived_z, "join_z", us=JOIN)
    second = [in_plane(rest, x, y, 0) for x, y in chips[1:3]]
    if len(CORNER) < 3:
        corner.append(in_plane(arrived_z[2], 1, 1, 0))
    first = near + [in_plane(block, 0, 0, 1) for block in near]
    half = len(near) * rows
    count = 2 * half
    up, gain, down = expert_up[0], moe_gain[None], expert_down[0]
    total, squares, route, hidden = call(
        functools.partial(first_up_kernel, "exp", len(first)),
        [((count, units), F32), ((count, 1), F32), ((rows, 1), F32), (wide, BF16)],
        [*first, up, gain, expert_ids[0].T, gate_weight[0].T],
        "up_first",
        scratch=[
            pltpu.VMEM((2, rows), jnp.int32), pltpu.VMEM((2, rows), F32),
            pltpu.VMEM((count, width), BF16), pltpu.SemaphoreType.DMA((3,)),
        ],
        in_hbm=range(len(first) + 2, len(first) + 4),
        out_hbm=(3,),
        limit=32,
    )
    *others, total = lax.optimization_barrier((*second, *corner, total))
    second = [rest, *others[:2], joined(others[2:], "join_corner", us=10.0)]
    activated = []
    for i, blocks in enumerate((second, [in_plane(block, 0, 0, 1) for block in second])):
        activated += call(
            functools.partial(second_up_kernel, "exp", len(blocks), slice(i * half, (i + 1) * half), model),
            [((half, units), BF16)],
            [*blocks, total, squares, up, gain],
            "up_second",
            scratch=[pltpu.VMEM((half, width), BF16)],
            limit=24,
            after=activated,
        )
    keep = rows // experts
    middle = model * 4 // 8
    cuts = (slice(0, middle), slice(middle, model))

    def down_part(i, columns, after, us=0.01):
        return call(
            functools.partial(down_kernel, columns),
            [((half, columns.stop - columns.start), BF16)],
            [activated[i], down],
            "down",
            after=after,
            us=us,
        )

    terms, mine, summed = [], None, None
    (sibling,) = down_part(1, cuts[0], [])
    for i, columns in enumerate(cuts):
        cut = columns.stop - columns.start
        if i:
            (mine,) = down_part(0, columns, summed[:1], us=0.01)
        else:
            mine, following = call(
                functools.partial(two_down_kernel, columns, cuts[1]),
                [((half, cut), BF16), ((half, cuts[1].stop - cuts[1].start), BF16)],
                [activated[0], activated[1], down],
                "down_two",
                after=[sibling],
            )
        summed = call(
            add_kernel, [((rows, cut), BF16)] * 4, [mine, in_plane(sibling, 0, 0, 1)], "add_cores"
        )
        sibling = following
        returned = [in_plane(summed[i], x, y, 0) for i, (x, y) in enumerate(chips) if i]
        slices = call(
            functools.partial(weigh_kernel, "exp"),
            [((rows, cut // experts), BF16)] * experts,
            [summed[0], *returned, route],
            "weigh",
            after=terms[2:3],
        )
        terms += [slices[0]] + [along_z(slices[k], k) for k in range(experts - 1, 0, -1)]
    (out,) = call(
        functools.partial(last_kernel, experts), [((rows // experts, model), BF16)], terms, "last"
    )
    return (hidden[None], out[None])


def solution(mesh):
    placed = (
        P("dp", "ctx", "exp"),
        P("dp", "ctx", "exp"),
        P("dp", "ctx", "exp"),
        P("dp", "ctx", None),
        P("dp", "ctx", None),
        P("dp", "ctx", "exp"),
        P("exp"),
        P("exp"),
        P("exp"),
        P(),
        P("dp", "ctx", None),
        P("dp", "ctx", None),
        P("exp", None, ("dp", "ctx")),
        P("exp", ("dp", "ctx"), None),
    )
    sizes = tuple(mesh.shape[axis] for axis in ("dp", "ctx", "exp"))
    return jax.shard_map(
        plane_body if sizes == (4, 2, 4) else body,
        mesh=mesh,
        in_specs=placed,
        out_specs=(P("dp", "ctx", "exp"), P("dp", ("ctx", "exp"), None)),
        check_vma=False,
    )
```

```python
import functools

import jax
import jax.numpy as jnp
from jax import lax
from jax.experimental import pallas as pl
from jax.experimental.pallas import tpu as pltpu
from jax.sharding import PartitionSpec as P

EPSILON = 1e-05
BF16 = jnp.bfloat16
CORNER = (1, 2)
JOIN = 10.0
F32 = jnp.float32
MIB = 1 << 20
EXACT = lax.Precision.HIGHEST
LAST = (((1,), (1,)), ((), ()))


def shifted(block, axis, distance):
    devices = range(lax.axis_size(axis))
    route = [(i - distance, i) for i in devices if i - distance in devices]
    return lax.ppermute(block, axis, route)


def route_slots(routes, experts):
    blocks = routes.shape[0]
    ordered = routes.reshape(blocks, -1)
    matches = (ordered[:, :, None] == jnp.arange(experts, dtype=jnp.int32)[None, None, :]).astype(
        jnp.int32
    )
    earlier = jnp.cumsum(matches, axis=1) - matches
    return jnp.sum(earlier * matches, axis=2).reshape(routes.shape)


def body(
    residual,
    ssm_input,
    ssm_gate,
    input_map,
    output_map,
    step_raw,
    log_rate,
    skip_gain,
    head_gain,
    moe_gain,
    expert_ids,
    gate_weight,
    expert_up,
    expert_down,
):
    heads_loc = log_rate.shape[0]
    local_rows = residual.shape[1]
    width_loc = residual.shape[2]
    head_size = width_loc // heads_loc
    values = ssm_input[0].astype(jnp.float32).reshape(local_rows, heads_loc, head_size)
    step_size = jax.nn.softplus(step_raw[0])
    cumulative = jnp.cumsum(step_size * (-jnp.exp(log_rate))[None, :], axis=0)
    scores = jnp.einsum(
        "tn,sn->ts", output_map[0], input_map[0], preferred_element_type=jnp.float32
    )
    positions = jnp.arange(local_rows)
    causal = positions[:, None] >= positions[None, :]
    spread = cumulative[:, None, :] - cumulative[None, :, :]
    kernel = (
        jnp.where(causal[:, :, None], jnp.exp(jnp.minimum(spread, 0.0)), 0.0)
        * scores[:, :, None]
        * step_size[None, :, :]
    )
    within = jnp.einsum("tsh,shp->thp", kernel, values, precision=lax.Precision.HIGHEST)
    ending = cumulative[-1]
    carried = jnp.exp(ending[None, :] - cumulative) * step_size
    in_map_wide = input_map[0].astype(jnp.float32)
    out_map_wide = output_map[0].astype(jnp.float32)
    local_state = jnp.einsum(
        "sh,shp,sn->hpn", carried, values, in_map_wide, precision=lax.Precision.HIGHEST
    )
    total_decay = jnp.exp(ending)
    incoming = jnp.zeros_like(local_state)
    for repeat in range(lax.axis_size("ctx") - 1):
        outgoing = total_decay[:, None, None] * incoming + local_state
        incoming = shifted(outgoing.astype(jnp.bfloat16), "ctx", 1).astype(outgoing.dtype)
    across_heads = (
        jnp.einsum("tn,hpn->thp", out_map_wide, incoming, precision=lax.Precision.HIGHEST)
        * jnp.exp(cumulative)[:, :, None]
    )
    mixed_y = within + across_heads + skip_gain[None, :, None] * values
    gated = mixed_y * jax.nn.silu(
        ssm_gate[0].astype(jnp.float32).reshape(local_rows, heads_loc, head_size)
    )
    normed = (
        gated
        * lax.rsqrt(jnp.mean(gated * gated, axis=2, keepdims=True) + EPSILON)
        * head_gain.reshape(heads_loc, head_size)
    )
    hidden = (residual[0].astype(jnp.float32) + normed.reshape(local_rows, width_loc)).astype(
        jnp.bfloat16
    )
    exp_count = lax.axis_size("exp")
    my_expert = lax.axis_index("exp")
    tok_rows = local_rows // exp_count
    capacity = min(tok_rows, max(4, 4 * tok_rows // exp_count))
    model_width = width_loc * exp_count
    routes_all = expert_ids[0].reshape(exp_count, tok_rows, 2)
    slots_all = route_slots(routes_all, exp_count)
    targets_all = routes_all * capacity + slots_all
    slot_ids = jnp.arange(exp_count * capacity, dtype=jnp.int32)
    own_targets = lax.dynamic_slice_in_dim(targets_all, my_expert, 1, 0)[0]
    own_weights = lax.dynamic_slice_in_dim(
        gate_weight[0].reshape(exp_count, tok_rows, 2), my_expert, 1, 0
    )[0]
    hidden_wide = hidden.astype(jnp.float32)
    squared_values = lax.psum(jnp.sum(hidden_wide * hidden_wide, axis=1), "exp")
    gain_part = lax.dynamic_slice_in_dim(moe_gain, my_expert * width_loc, width_loc, 0)
    normal_part = (
        hidden_wide
        * lax.rsqrt(squared_values[:, None] / model_width + EPSILON)
        * gain_part[None, :]
    ).astype(jnp.bfloat16)
    placing_all = jnp.any(
        slot_ids[None, :, None, None] == targets_all[:, None, :, :], axis=3
    ).astype(jnp.bfloat16)
    outbound = jnp.einsum(
        "bqt,btc->bqc",
        placing_all,
        normal_part.reshape(exp_count, tok_rows, width_loc),
        preferred_element_type=jnp.float32,
    )
    outbound = outbound.astype(jnp.bfloat16).reshape(exp_count, exp_count, capacity, width_loc)
    arrived = lax.all_to_all(outbound, "exp", split_axis=1, concat_axis=3, tiled=True).reshape(
        exp_count * capacity, model_width
    )
    up_local = expert_up[0]
    down_local = expert_down[0]
    activated = jax.nn.silu(
        jnp.dot(
            lax.all_gather(arrived, ("dp", "ctx"), axis=0, tiled=True),
            up_local,
            preferred_element_type=jnp.float32,
        )
    ).astype(jnp.bfloat16)
    summed = lax.psum_scatter(
        jnp.dot(activated, down_local, preferred_element_type=jnp.float32).astype(jnp.bfloat16),
        ("dp", "ctx"),
        scatter_dimension=0,
        tiled=True,
    )
    sent_back = summed.reshape(exp_count, capacity, model_width)
    returned = lax.all_to_all(sent_back, "exp", split_axis=0, concat_axis=0, tiled=True).reshape(
        exp_count * capacity, model_width
    )
    picking = (own_targets.reshape(-1)[:, None] == slot_ids[None, :]).astype(jnp.bfloat16)
    chosen = jnp.dot(picking, returned, preferred_element_type=jnp.float32).reshape(
        tok_rows, 2, model_width
    )
    combined = jnp.sum(own_weights[:, :, None] * chosen, axis=1).astype(jnp.bfloat16)
    return (hidden[None], combined[None])


def softplus(raw):
    return jnp.maximum(raw, 0.0) + jnp.log1p(jnp.exp(-jnp.abs(raw)))


def iotas(rows, columns):
    shape = (rows, columns)
    return lax.broadcasted_iota(jnp.int32, shape, 0), lax.broadcasted_iota(jnp.int32, shape, 1)


def as_column(row):
    size = row.shape[1]
    down, across = iotas(size, size)
    return jnp.sum(jnp.where(down == across, row, 0.0), axis=1, keepdims=True)


def fetch(pairs, sems):
    copies = [pltpu.make_async_copy(a, b, sems.at[i]) for i, (a, b) in enumerate(pairs)]
    for copy in copies:
        copy.start()
    return copies


def pack_kernel(b_hbm, step_hbm, out_ref, b_ref, step_ref, sems):
    copies = fetch([(b_hbm, b_ref), (step_hbm, step_ref)], sems)
    rows, (heads, places) = b_ref.shape[0], step_ref.shape
    out_ref[rows:] = jnp.zeros((heads, out_ref.shape[1]), F32)
    for copy in copies:
        copy.wait()
    out_ref[:rows] = b_ref[...].astype(F32)
    out_ref[rows:, :places] = step_ref[...]


def own_kernel(
    x_hbm, gate_hbm, res_hbm, b_hbm, c_hbm, step_hbm, rate_hbm, gain_hbm, skip_hbm,
    mixed_ref, gate_ref, decay_ref, res_ref, c_ref, rate_ref, gain_ref,
    x_ref, raw_gate_ref, b_ref, step_ref, skip_ref, sems,
):
    copies = fetch(
        [
            (step_hbm, step_ref), (rate_hbm, rate_ref), (b_hbm, b_ref), (c_hbm, c_ref), (x_hbm, x_ref),
            (skip_hbm, skip_ref), (gate_hbm, raw_gate_ref), (res_hbm, res_ref), (gain_hbm, gain_ref),
        ],
        sems,
    )
    rows, width = x_ref.shape
    heads = step_ref.shape[0]
    size = width // heads
    pad = 64 - rows
    copies[0].wait()
    copies[1].wait()
    steps = softplus(step_ref[...])
    decay = steps * -jnp.exp(as_column(rate_ref[...]))
    down, across = iotas(rows, 128)
    place = across & 63
    to_row = jnp.where((down <= place) & (place < rows), -1.0, 0.0)
    to_step = jnp.where(down == place, 1.0, 0.0)
    row_part = jnp.dot(decay, to_row, precision=EXACT, preferred_element_type=F32)
    steps_twice = jnp.dot(steps, to_step, precision=EXACT, preferred_element_type=F32)
    t_row, u_col = iotas(rows, rows)
    to_col = jnp.where(u_col <= t_row, 1.0, 0.0)
    col_part = lax.dot_general(to_col, decay, LAST, precision=EXACT, preferred_element_type=F32)
    copies[2].wait()
    copies[3].wait()
    zeros = jnp.zeros((pad, b_ref.shape[1]), BF16)
    maps = jnp.concatenate([b_ref[...], zeros, b_ref[...], zeros], axis=0)
    scores = lax.dot_general(c_ref[...], maps, LAST, preferred_element_type=F32)
    scores = jnp.where(place <= down, scores, 0.0)
    lane = lax.broadcasted_iota(jnp.int32, (1, 128), 1)
    low = lane < size
    zeros = jnp.zeros((pad, 128), BF16)
    for copy in copies[4:]:
        copy.wait()
    skips = as_column(skip_ref[...])
    for pair in range(width // 128):
        cut = slice(pair * 128, (pair + 1) * 128)
        first, second = 2 * pair, 2 * pair + 1
        x_own = x_ref[:, cut]
        column = jnp.where(low, col_part[:, first : first + 1], col_part[:, second : second + 1])
        row = jnp.where(low, row_part[first : first + 1], row_part[second : second + 1])
        step = jnp.where(low, steps_twice[first : first + 1], steps_twice[second : second + 1])
        gap = jnp.where(place == down, 0.0, jnp.minimum(column + row, 0.0))
        kernel = jnp.exp(gap) * scores * step
        high = kernel.astype(BF16)
        rest = (kernel - high.astype(F32)).astype(BF16)
        none = jnp.zeros_like(x_own)
        values = jnp.concatenate(
            [jnp.where(low, x_own, none), zeros, jnp.where(low, none, x_own), zeros], axis=0
        )
        mixed = jnp.dot(jnp.concatenate([high, rest], axis=0), values, preferred_element_type=F32)
        skip = jnp.where(low, skips[first : first + 1], skips[second : second + 1])
        mixed_ref[:, cut] = mixed[:rows] + mixed[rows:] + skip * x_own.astype(F32)
        gate = raw_gate_ref[:, cut].astype(F32)
        gate_ref[:, cut] = gate / (1.0 + jnp.exp(-gate))
        decay_ref[:, cut] = jnp.exp(column)


def mixer_kernel(
    mixed_ref, gate_ref, decay_ref, res_ref, c_ref, rate_ref, gain_ref, x_ref, pack_ref, out_ref
):
    rows, width = x_ref.shape
    heads = rate_ref.shape[1]
    size = width // heads
    steps = softplus(pack_ref[rows:, :rows])
    decay = steps * -jnp.exp(as_column(rate_ref[...]))
    down, across = iotas(rows, rows)
    after = jnp.where(down > across, 1.0, 0.0)
    same = jnp.where(down == across, 1.0, 0.0)
    carried = jnp.exp(jnp.dot(decay, after, precision=EXACT, preferred_element_type=F32)) * steps
    carried = lax.dot_general(same, carried, LAST, precision=EXACT, preferred_element_type=F32)
    scores = lax.dot_general(
        c_ref[...], pack_ref[:rows].astype(BF16), LAST, preferred_element_type=F32
    )
    s_high = scores.astype(BF16)
    s_rest = (scores - s_high.astype(F32)).astype(BF16)
    s_both = jnp.concatenate([s_high, s_rest], axis=0)
    low = lax.broadcasted_iota(jnp.int32, (1, 128), 1) < size
    for pair in range(width // 128):
        cut = slice(pair * 128, (pair + 1) * 128)
        first, second = 2 * pair, 2 * pair + 1
        weight = jnp.where(low, carried[:, first : first + 1], carried[:, second : second + 1])
        values = weight * x_ref[:, cut].astype(F32)
        v_high = values.astype(BF16)
        v_rest = (values - v_high.astype(F32)).astype(BF16)
        cross = jnp.dot(s_both, v_high, preferred_element_type=F32)
        cross = cross[:rows] + cross[rows:] + jnp.dot(s_high, v_rest, preferred_element_type=F32)
        gated = (mixed_ref[:, cut] + decay_ref[:, cut] * cross) * gate_ref[:, cut]
        square = gated * gated
        mean_low = jnp.sum(jnp.where(low, square, 0.0), axis=1, keepdims=True) / size
        mean_high = jnp.sum(jnp.where(low, 0.0, square), axis=1, keepdims=True) / size
        scale = lax.rsqrt(jnp.where(low, mean_low, mean_high) + EPSILON)
        normed = gated * scale * gain_ref[:, cut]
        out_ref[:, cut] = (res_ref[:, cut].astype(F32) + normed).astype(BF16)


def add_up(blocks, gain, weights, scaled):
    rows, width = blocks[0].shape
    squares = []
    for i, block in enumerate(blocks):
        wide = block[...].astype(F32)
        squares.append(jnp.sum(wide * wide, axis=1, keepdims=True))
        scaled[i * rows : (i + 1) * rows] = (wide * gain).astype(BF16)
    return jnp.dot(scaled[...], weights, preferred_element_type=F32), jnp.concatenate(squares, axis=0)


def slice_of(expert, k, up_ref, gain_ref, width):
    cut = pl.ds(pl.multiple_of((lax.axis_index(expert) ^ k) * width, width), width)
    return gain_ref[:, cut], up_ref[cut]


def first_up_kernel(expert, count, *refs):
    blocks, (up_ref, gain_ref, ids_hbm, weight_hbm) = refs[:count], refs[count : count + 4]
    total_ref, square_ref, route_ref, hidden_hbm = refs[count + 4 : count + 8]
    ids, weights, scaled, sems = refs[count + 8 :]
    copies = fetch([(ids_hbm, ids), (weight_hbm, weights), (blocks[0], hidden_hbm)], sems)
    width = blocks[0].shape[1]
    gain, up = slice_of(expert, 0, up_ref, gain_ref, width)
    total_ref[...], square_ref[...] = add_up(blocks, gain, up, scaled)
    for copy in copies:
        copy.wait()
    row = jnp.sum(
        jnp.where(ids[...] == lax.axis_index(expert), weights[...], 0.0), axis=0, keepdims=True
    )
    route_ref[...] = as_column(row)


def second_up_kernel(expert, count, rows, model, *refs):
    blocks = refs[:count]
    total_ref, square_ref, up_ref, gain_ref, out_ref, scaled = refs[count:]
    width = scaled.shape[1]
    total, squares = total_ref[rows], square_ref[rows]
    for k in range(1, model // width):
        cut = slice((k - 1) * width, k * width)
        gain, up = slice_of(expert, k, up_ref, gain_ref, width)
        part, square = add_up([b.at[:, cut] for b in blocks], gain, up, scaled)
        total += part
        squares += square
    value = total * lax.rsqrt(squares / model + EPSILON)
    out_ref[...] = (value / (1.0 + jnp.exp(-value))).astype(BF16)


def down_kernel(columns, act_ref, down_ref, out_ref):
    out_ref[...] = jnp.dot(
        act_ref[...], down_ref[:, columns], preferred_element_type=F32
    ).astype(BF16)


def two_down_kernel(own_columns, other_columns, own_ref, other_ref, down_ref, own_out_ref, other_out_ref):
    down_kernel(other_columns, other_ref, down_ref, other_out_ref)
    down_kernel(own_columns, own_ref, down_ref, own_out_ref)


def join_kernel(*refs):
    blocks, out_ref = refs[:-1], refs[-1]
    width = blocks[0].shape[1]
    for i, block in enumerate(blocks):
        out_ref[:, i * width : (i + 1) * width] = block[...]


def add_kernel(own_ref, other_ref, *outs):
    rows = outs[0].shape[0]
    for i, out in enumerate(outs):
        cut = slice(i * rows, (i + 1) * rows)
        out[...] = (own_ref[cut].astype(F32) + other_ref[cut].astype(F32)).astype(BF16)


def weigh_kernel(expert, own_ref, *refs):
    others, route_ref, outs = refs[:3], refs[3], refs[4:]
    me = lax.axis_index(expert)
    rows, columns = own_ref.shape
    parts = len(outs)
    keep, width = rows // parts, columns // parts
    total = own_ref[...].astype(F32)
    for other in others:
        total += other[...].astype(F32)
    total = (total * route_ref[...]).astype(BF16)
    place, source = iotas(parts * rows, parts * rows)
    part, place = place // rows, place % rows
    wanted = place // keep * rows + (part ^ me) * keep + place % keep
    stacked = jnp.concatenate([total[:, j * width : (j + 1) * width] for j in range(parts)], axis=0)
    pick = jnp.where(source == wanted, 1.0, 0.0).astype(BF16)
    picked = jnp.dot(pick, stacked, preferred_element_type=F32)
    for k, out in enumerate(outs):
        out[...] = picked[k * rows : (k + 1) * rows].astype(BF16)


def last_kernel(count, *refs):
    terms, out_ref = refs[:-1], refs[-1]
    keep, start = out_ref.shape[0], 0
    for i in range(0, len(terms), count):
        total = sum(term[...].astype(F32) for term in terms[i : i + count])
        width = total.shape[1]
        for j in range(count):
            out_ref[:, start : start + width] = total[j * keep : (j + 1) * keep].astype(BF16)
            start += width


def call(kernel, outs, inputs, name, scratch=(), in_hbm=(), out_hbm=(), limit=16, us=0.01, after=()):
    vmem, hbm = pl.BlockSpec(memory_space=pltpu.VMEM), pl.BlockSpec(memory_space=pltpu.HBM)
    inputs = [
        pltpu.with_memory_space_constraint(a, pltpu.HBM) if i in in_hbm else a for i, a in enumerate(inputs)
    ]
    given, extra = len(inputs), len(after)

    def without(*refs):
        return kernel(*refs[:given], *refs[given + extra :])

    return pl.pallas_call(
        without,
        out_shape=[jax.ShapeDtypeStruct(shape, dtype) for shape, dtype in outs],
        in_specs=[hbm if i in in_hbm else vmem for i in range(given)]
        + [pl.BlockSpec(memory_space=pl.ANY)] * extra,
        out_specs=[hbm if i in out_hbm else vmem for i in range(len(outs))],
        scratch_shapes=scratch,
        compiler_params=pltpu.CompilerParams(vmem_limit_bytes=limit * MIB),
        cost_estimate=pl.CostEstimate(
            flops=int(us * 1e9), bytes_accessed=int(us * 3e6), transcendentals=0
        ),
        name=name,
    )(*inputs, *after)


def plane_body(
    residual, ssm_input, ssm_gate, input_map, output_map, step_raw, log_rate, skip_gain, head_gain,
    moe_gain, expert_ids, gate_weight, expert_up, expert_down,
):
    rows, width = residual.shape[1:]
    heads = log_rate.shape[0]
    state = input_map.shape[2]
    experts = lax.axis_size("exp")
    model = experts * width
    units = expert_up.shape[2]
    plane = ("dp", "ctx")

    def along_z(block, k):
        return lax.ppermute(block, "exp", [(i, i ^ k) for i in range(experts)])

    def in_plane(block, x, y, core):
        route = [
            (d * 2 + c, (d ^ (y * 2) ^ core) * 2 + (c ^ x)) for d in range(4) for c in range(2)
        ]
        return lax.ppermute(block, plane, route)

    step_t = step_raw[0].T
    (packed,) = call(
        pack_kernel,
        [((rows + heads, state), F32)],
        [input_map[0], step_t],
        "pack",
        scratch=[
            pltpu.VMEM((rows, state), BF16), pltpu.VMEM((heads, rows), F32), pltpu.SemaphoreType.DMA((2,)),
        ],
        in_hbm=range(2),
    )
    before = [lax.ppermute(a, "ctx", [(0, 1)]) for a in (ssm_input[0], packed)]
    wide, flat = (rows, width), (rows, state)
    own = call(
        own_kernel,
        [(wide, F32), (wide, F32), (wide, F32), (wide, BF16), (flat, BF16), ((1, heads), F32), ((1, width), F32)],
        [
            ssm_input[0], ssm_gate[0], residual[0], input_map[0], output_map[0], step_t,
            log_rate[None], head_gain[None], skip_gain[None],
        ],
        "mixer_own",
        scratch=[
            pltpu.VMEM(wide, BF16), pltpu.VMEM(wide, BF16), pltpu.VMEM(flat, BF16),
            pltpu.VMEM((heads, rows), F32), pltpu.VMEM((1, heads), F32), pltpu.SemaphoreType.DMA((9,)),
        ],
        in_hbm=range(9),
    )
    (sent,) = call(mixer_kernel, [(wide, BF16)], [*own, *before], "mixer")
    chips = ((0, 0), (1, 0), (0, 1), (1, 1))

    def joined(blocks, name, after=(), us=0.01):
        shape = (rows, width * len(blocks))
        return call(join_kernel, [(shape, BF16)], blocks, name, after=after, us=us)[0]

    arrived_z = [along_z(sent, k) for k in range(1, experts)]
    near = [sent] + [in_plane(sent, x, y, 0) for x, y in chips[1:]]
    corner = [along_z(near[3], k) for k in CORNER]
    rest = joined(arrived_z, "join_z", us=JOIN)
    second = [in_plane(rest, x, y, 0) for x, y in chips[1:3]]
    if len(CORNER) < 3:
        corner.append(in_plane(arrived_z[2], 1, 1, 0))
    first = near + [in_plane(block, 0, 0, 1) for block in near]
    half = len(near) * rows
    count = 2 * half
    up, gain, down = expert_up[0], moe_gain[None], expert_down[0]
    total, squares, route, hidden = call(
        functools.partial(first_up_kernel, "exp", len(first)),
        [((count, units), F32), ((count, 1), F32), ((rows, 1), F32), (wide, BF16)],
        [*first, up, gain, expert_ids[0].T, gate_weight[0].T],
        "up_first",
        scratch=[
            pltpu.VMEM((2, rows), jnp.int32), pltpu.VMEM((2, rows), F32),
            pltpu.VMEM((count, width), BF16), pltpu.SemaphoreType.DMA((3,)),
        ],
        in_hbm=range(len(first) + 2, len(first) + 4),
        out_hbm=(3,),
        limit=32,
    )
    *others, total = lax.optimization_barrier((*second, *corner, total))
    second = [rest, *others[:2], joined(others[2:], "join_corner", us=10.0)]
    activated = []
    for i, blocks in enumerate((second, [in_plane(block, 0, 0, 1) for block in second])):
        activated += call(
            functools.partial(second_up_kernel, "exp", len(blocks), slice(i * half, (i + 1) * half), model),
            [((half, units), BF16)],
            [*blocks, total, squares, up, gain],
            "up_second",
            scratch=[pltpu.VMEM((half, width), BF16)],
            limit=24,
            after=activated,
        )
    keep = rows // experts
    middle = model * 4 // 8
    cuts = (slice(0, middle), slice(middle, model))

    def down_part(i, columns, after, us=0.01):
        return call(
            functools.partial(down_kernel, columns),
            [((half, columns.stop - columns.start), BF16)],
            [activated[i], down],
            "down",
            after=after,
            us=us,
        )

    terms, mine, summed = [], None, None
    (sibling,) = down_part(1, cuts[0], [])
    for i, columns in enumerate(cuts):
        cut = columns.stop - columns.start
        if i:
            (mine,) = down_part(0, columns, summed[:1], us=0.01)
        else:
            mine, following = call(
                functools.partial(two_down_kernel, columns, cuts[1]),
                [((half, cut), BF16), ((half, cuts[1].stop - cuts[1].start), BF16)],
                [activated[0], activated[1], down],
                "down_two",
                after=[sibling],
            )
        summed = call(
            add_kernel, [((rows, cut), BF16)] * 4, [mine, in_plane(sibling, 0, 0, 1)], "add_cores"
        )
        sibling = following
        returned = [in_plane(summed[i], x, y, 0) for i, (x, y) in enumerate(chips) if i]
        slices = call(
            functools.partial(weigh_kernel, "exp"),
            [((rows, cut // experts), BF16)] * experts,
            [summed[0], *returned, route],
            "weigh",
            after=terms[2:3],
        )
        terms += [slices[0]] + [along_z(slices[k], k) for k in range(experts - 1, 0, -1)]
    (out,) = call(
        functools.partial(last_kernel, experts), [((rows // experts, model), BF16)], terms, "last"
    )
    return (hidden[None], out[None])


def solution(mesh):
    placed = (
        P("dp", "ctx", "exp"),
        P("dp", "ctx", "exp"),
        P("dp", "ctx", "exp"),
        P("dp", "ctx", None),
        P("dp", "ctx", None),
        P("dp", "ctx", "exp"),
        P("exp"),
        P("exp"),
        P("exp"),
        P(),
        P("dp", "ctx", None),
        P("dp", "ctx", None),
        P("exp", None, ("dp", "ctx")),
        P("exp", ("dp", "ctx"), None),
    )
    sizes = tuple(mesh.shape[axis] for axis in ("dp", "ctx", "exp"))
    return jax.shard_map(
        plane_body if sizes == (4, 2, 4) else body,
        mesh=mesh,
        in_specs=placed,
        out_specs=(P("dp", "ctx", "exp"), P("dp", ("ctx", "exp"), None)),
        check_vma=False,
    )
```
